512 devices in a mesh: slide: 64 (over z, x, core), seq: 8 (over y).
Axes of the slice: x: 4, y: 8, z: 8, core: 2. Of those that a mesh axis runs over, the one named last changes fastest.
Arguments:
- queries: bfloat16 [131072, 768], P(('slide', 'seq')), may hold values from -120 to 120
- keys: bfloat16 [131072, 768], P(('slide', 'seq')), may hold values from -4 to 4
- values: bfloat16 [131072, 768], P(('slide', 'seq')), may hold values from -6 to 6
- grad_y: bfloat16 [131072, 768], P(('slide', 'seq')), may hold values from -24 to 24
- lengths: int32 [64], P('slide'), may hold values from 512 to 2048, as said below
- w_out: bfloat16 [768, 768], replicated, may hold values from -0.21875 to 0.21875
Outputs:
- output: bfloat16 [131072, 768], P(('slide', 'seq'))
- grad_q: bfloat16 [131072, 768], P(('slide', 'seq'))
- grad_k: bfloat16 [131072, 768], P(('slide', 'seq'))
- grad_v: bfloat16 [131072, 768], P(('slide', 'seq'))
- weight_grad: float32 [768, 768], P('seq', 'slide')
The draws below stay inside these ranges and needn't reach their ends.
Inputs may be any that keep to these rules, and one draw needn't show every extreme that they name: `lengths`: each slide's tile count; some slide holds all 2048 positions.
All inputs are finite; a program needn't handle non-finite values.
Results may differ from the reference program's by a relative error of at most 0.035.
Values may be sent and summed in bfloat16 or wider, within the bound.
A program may use at most 64 MiB of HBM per device.

```python
import jax
import jax.numpy as jnp
import numpy as np
from jax import lax

HEAD_COUNT = 12
HD = 64
D = 768
ROWS = 256
DILATION_STEP = 16
SLIDES = 64
LEN = 2048
TOKENS = 131072


def roll_slides(array_input, offset):
    shaped = array_input.reshape((SLIDES, LEN) + array_input.shape[1:])
    return jnp.roll(shaped, offset, axis=1).reshape(array_input.shape)


def shared_rows(key):
    base_rows = jnp.clip(jax.random.normal(key, (TOKENS, D), jnp.float32), -4.0, 4.0)
    picked = jax.random.randint(jax.random.fold_in(key, 91), (TOKENS, 1), 0, 64) == 0
    target_rows = roll_slides(base_rows, -(LEN // 2))
    return (base_rows, picked, target_rows)


def draw_queries(key, part):
    base_rows, picked, target_rows = shared_rows(key)
    key = jax.random.fold_in(key, 1)
    own_rows = jnp.clip(jax.random.normal(key, (TOKENS, D), jnp.float32), -4.0, 4.0)
    own_rows = jnp.where(picked, 3.0 * target_rows, own_rows)
    return own_rows.astype(jnp.bfloat16)


def draw_keys(key, part):
    base_rows, picked, target_rows = shared_rows(key)
    return base_rows.astype(jnp.bfloat16)


def draw_lengths(key, part):
    key = jax.random.fold_in(key, 3)
    counts = jax.random.randint(key, (SLIDES,), LEN // 4, LEN + 1)
    longest = jax.random.randint(jax.random.fold_in(key, 4), (), 0, SLIDES)
    return jnp.where(jnp.arange(SLIDES) == longest, LEN, counts).astype(jnp.int32)


def raised(drawn, key, source, target, parts, factor):
    def block_of(axis_at):
        return (jnp.arange(drawn.shape[axis_at]) // (drawn.shape[axis_at] // parts)).reshape((-1,) + (1,) * (drawn.ndim - 1 - axis_at))

    one_side = jax.random.permutation(key, parts)[block_of(target)]
    far = (block_of(target) + parts // 2) % parts
    return jnp.where((block_of(source) == one_side) | (block_of(source) == far), factor * drawn, drawn)


def steps_of(own_key, dims, shards, smallest, largest):
    loudness = 1.0
    for dim, parts in shards:
        heights = jax.random.uniform(jax.random.fold_in(jax.random.fold_in(own_key, 6), dim), (parts,), jnp.float32, smallest / len(shards), largest / len(shards))
        loudness = loudness * jnp.repeat(jnp.exp(heights), dims[dim] // parts).reshape((-1,) + (1,) * (len(dims) - 1 - dim))
    return loudness


def gaussian(stream_key, extent, deviation, limit, split=(), kind=jnp.bfloat16):
    drawn = deviation * jax.random.normal(stream_key, extent, jnp.float32)
    if split:
        drawn = drawn * steps_of(stream_key, extent, split, -0.22, 0.18)
    return jnp.clip(drawn, -limit, limit).astype(kind)


def heavy_noise(rng, dims, deviation, reach, shards, heavy, kind=jnp.bfloat16):
    values = deviation * jax.random.normal(rng, dims, jnp.float32)
    if shards:
        values = values * steps_of(rng, dims, shards, -0.22, 0.18)
    return jnp.clip(raised(values, jax.random.fold_in(rng, 3), *heavy), -reach, reach).astype(kind)


def setup_inputs(seed: int = 0) -> dict:
    arg_keys = jax.random.split(jax.random.key(seed), 7)
    queries = draw_queries(jax.random.fold_in(arg_keys[6], 71), 0)
    keys = draw_keys(jax.random.fold_in(arg_keys[6], 71), 0)
    values = gaussian(arg_keys[2], (TOKENS, D), 1.0, 6.0, ((0, 512),))
    grad_y = heavy_noise(arg_keys[3], (TOKENS, D), 1.0, 24.0, ((0, 512),), (0, 1, 256, 6.0))
    lengths = draw_lengths(jax.random.fold_in(arg_keys[6], 71), 0)
    w_out = gaussian(arg_keys[5], (D, D), D ** -0.5, 0.21875)
    return {"queries": queries, "keys": keys, "values": values, "grad_y": grad_y, "lengths": lengths, "w_out": w_out}


masked_score = -1e30


def pick_rows(array_input):
    reshaped_rows = array_input.reshape((array_input.shape[0] // DILATION_STEP, DILATION_STEP) + array_input.shape[1:])
    return reshaped_rows[:, np.arange(HEAD_COUNT) % DILATION_STEP, np.arange(HEAD_COUNT)]


def spread_rows(array_input, filler):
    choose_rows = np.arange(DILATION_STEP)[:, None] == (np.arange(HEAD_COUNT) % DILATION_STEP)[None, :]
    choose_rows = choose_rows.reshape((1, DILATION_STEP, HEAD_COUNT) + (1,) * (array_input.ndim - 2))
    scatter_rows = jnp.where(choose_rows, array_input[:, None], jnp.asarray(filler, array_input.dtype))
    return scatter_rows.reshape((array_input.shape[0] * DILATION_STEP,) + array_input.shape[1:])


def round_half(array_input):
    return lax.optimization_barrier(array_input.astype(jnp.bfloat16)).astype(jnp.float32)


def slide_pass(query_in, key_in, value_in, grad_in, length, w_out):
    score_scale = HD ** -0.5
    total_len = query_in.shape[0]
    groups = total_len // ROWS
    q_heads = query_in.reshape(total_len, HEAD_COUNT, HD).astype(jnp.float32)
    k_heads = key_in.reshape(total_len, HEAD_COUNT, HD).astype(jnp.float32)
    v_heads = value_in.reshape(total_len, HEAD_COUNT, HD).astype(jnp.float32)
    position = jnp.arange(total_len, dtype=jnp.int32)
    row_valid = position < length
    valid_grp = row_valid.reshape(groups, ROWS)
    q_grp = q_heads.reshape(groups, ROWS, HEAD_COUNT, HD)
    k_grp = k_heads.reshape(groups, ROWS, HEAD_COUNT, HD)
    v_grp = v_heads.reshape(groups, ROWS, HEAD_COUNT, HD)
    key_ok = valid_grp[:, None, None, :]
    dense_score = jnp.einsum('gihd,gjhd->ghij', q_grp, k_grp) * score_scale
    dense_score = jnp.where(key_ok, dense_score, masked_score)
    dense_max = dense_score.max(-1)
    q_sel = pick_rows(q_heads)
    k_sel = pick_rows(k_heads)
    v_sel = pick_rows(v_heads)
    sel_valid = pick_rows(jnp.broadcast_to(row_valid[:, None], (total_len, HEAD_COUNT)))
    key_sparse = sel_valid.T[:, None, :]
    sparse_score = jnp.einsum('ahd,bhd->hab', q_sel, k_sel) * score_scale
    sparse_score = jnp.where(key_sparse, sparse_score, masked_score)
    sparse_max = sparse_score.max(-1)
    row_max = jnp.maximum(dense_max.transpose(0, 2, 1).reshape(total_len, HEAD_COUNT),
                          spread_rows(sparse_max.T, masked_score))
    max_grp = row_max.reshape(groups, ROWS, HEAD_COUNT).transpose(0, 2, 1)
    max_sel = pick_rows(row_max)
    dense_exp = jnp.where(key_ok, jnp.exp(dense_score - max_grp[..., None]), 0.0)
    sparse_exp = jnp.where(key_sparse, jnp.exp(sparse_score - max_sel.T[:, :, None]), 0.0)
    row_total = dense_exp.sum(-1).transpose(0, 2, 1).reshape(total_len, HEAD_COUNT) + spread_rows(sparse_exp.sum(-1).T, 0.0)
    row_total = jnp.where(row_valid[:, None], row_total, 1.0)
    total_grp = row_total.reshape(groups, ROWS, HEAD_COUNT).transpose(0, 2, 1)
    total_sel = pick_rows(row_total)
    dense_prob = jnp.where(valid_grp[:, None, :, None], dense_exp / total_grp[..., None], 0.0)
    sparse_prob = jnp.where(sel_valid.T[:, :, None], sparse_exp / total_sel.T[:, :, None], 0.0)
    dense_half = round_half(dense_prob)
    sparse_half = round_half(sparse_prob)
    dense_out = jnp.einsum('ghij,gjhd->gihd', dense_half, v_grp).reshape(total_len, HEAD_COUNT, HD)
    sparse_out = jnp.einsum('hab,bhd->ahd', sparse_half, v_sel)
    attended = (dense_out + spread_rows(sparse_out, 0.0)).astype(jnp.bfloat16)
    attn_flat = attended.reshape(total_len, D)
    output = jnp.dot(attn_flat, w_out, preferred_element_type=jnp.float32).astype(jnp.bfloat16)
    grad_attn = jnp.dot(grad_in, w_out.T, preferred_element_type=jnp.float32).astype(jnp.bfloat16)
    weight_part = jnp.dot(attn_flat.T, grad_in, preferred_element_type=jnp.float32)
    grad_heads = grad_attn.reshape(total_len, HEAD_COUNT, HD).astype(jnp.float32)
    row_dot = jnp.sum(grad_heads * attended.astype(jnp.float32).reshape(total_len, HEAD_COUNT, HD), axis=-1)
    dot_grp = row_dot.reshape(groups, ROWS, HEAD_COUNT).transpose(0, 2, 1)
    grad_grp = grad_heads.reshape(groups, ROWS, HEAD_COUNT, HD)
    dense_dprob = jnp.einsum('gihd,gjhd->ghij', grad_grp, v_grp)
    dense_dscore = round_half(dense_prob * (dense_dprob - dot_grp[..., None]))
    grad_q_dense = jnp.einsum('ghij,gjhd->gihd', dense_dscore, k_grp) * score_scale
    grad_k_dense = jnp.einsum('ghij,gihd->gjhd', dense_dscore, q_grp) * score_scale
    grad_v_dense = jnp.einsum('ghij,gihd->gjhd', dense_half, grad_grp)
    grad_sel = pick_rows(grad_heads)
    dot_sel = pick_rows(row_dot)
    sparse_dprob = jnp.einsum('ahd,bhd->hab', grad_sel, v_sel)
    sparse_dscore = round_half(sparse_prob * (sparse_dprob - dot_sel.T[:, :, None]))
    grad_q_sparse = jnp.einsum('hab,bhd->ahd', sparse_dscore, k_sel) * score_scale
    grad_k_sparse = jnp.einsum('hab,ahd->bhd', sparse_dscore, q_sel) * score_scale
    grad_v_sparse = jnp.einsum('hab,ahd->bhd', sparse_half, grad_sel)
    grad_q = (grad_q_dense.reshape(total_len, HEAD_COUNT, HD) + spread_rows(grad_q_sparse, 0.0)).astype(jnp.bfloat16)
    grad_k = (grad_k_dense.reshape(total_len, HEAD_COUNT, HD) + spread_rows(grad_k_sparse, 0.0)).astype(jnp.bfloat16)
    grad_v = (grad_v_dense.reshape(total_len, HEAD_COUNT, HD) + spread_rows(grad_v_sparse, 0.0)).astype(jnp.bfloat16)
    return (output, grad_q.reshape(total_len, D), grad_k.reshape(total_len, D),
            grad_v.reshape(total_len, D), weight_part)


def reference(queries, keys, values, grad_y, lengths, w_out):
    def one_slide(weight_acc, inputs):
        query_in, key_in, value_in, grad_in, length = inputs
        output, grad_q, grad_k, grad_v, weight_part = slide_pass(query_in, key_in, value_in, grad_in, length, w_out)
        return weight_acc + weight_part, (output, grad_q, grad_k, grad_v)

    inputs = (queries.reshape(SLIDES, LEN, D), keys.reshape(SLIDES, LEN, D), values.reshape(SLIDES, LEN, D),
              grad_y.reshape(SLIDES, LEN, D), lengths)
    weight_grad, stacked = lax.scan(one_slide, jnp.zeros((D, D), jnp.float32), inputs)
    output, grad_q, grad_k, grad_v = stacked
    return (output.reshape(TOKENS, D), grad_q.reshape(TOKENS, D), grad_k.reshape(TOKENS, D),
            grad_v.reshape(TOKENS, D), weight_grad)
```

```python
import functools

import jax
import jax.numpy as jnp
from jax import lax
from jax.experimental import pallas as pl
from jax.experimental.pallas import tpu as pltpu
from jax.sharding import PartitionSpec as P

HEADS = 12
HD = 64
D = 768
ROWS = 256
STEP = 16
PICK = ROWS // STEP
COMPACT = HEADS * PICK
NY, NZ, NX = 8, 8, 4
FAR = NY * PICK
SCALE = HD**-0.5
NEG = -1e30
MESH = pl.DeviceIdType.MESH
bf16 = jnp.bfloat16
f32 = jnp.float32


def nn(a, b):
    return lax.dot_general(a, b, (((1,), (0,)), ((), ())), preferred_element_type=f32)


def nt(a, b):
    return lax.dot_general(a, b, (((1,), (1,)), ((), ())), preferred_element_type=f32)


def iota(shape, dim):
    return lax.broadcasted_iota(jnp.int32, shape, dim)


def half(cond):
    return jnp.where(cond, 1.0, 0.0).astype(bf16)


def kernel(
    len_ref, q_ref, k_ref, v_ref, gy_ref, w_ref,
    out_ref, gq_ref, gk_ref, gv_ref, wg_ref,
    kv_all, qg_all, aug_all, gyt, atth, att_far,
    grad, att, vt, kt, gk_acc, gv_acc,
    w_full, wy, wz, wx, r1y, r1z, r1x,
    a0, a1, a2, r20, r21, r22, s3, r3,
    kv_s, kv_r, qg_s, qg_r, aug_s, aug_r, core_s, core_r,
    y_s, y_r, z_s, z_r, x_s, x_r,
    b0_s, b0_r, b1_s, b1_r, b2_s, b2_r, f_s, f_r,
):
    slide = lax.axis_index("slide")
    y = lax.axis_index("seq")
    c = lax.rem(slide, 2)
    x = lax.rem(slide // 2, NX)
    z = slide // (2 * NX)

    def device(z_at, x_at, c_at, y_at):
        return ((z_at * NX + x_at) * 2 + c_at, y_at)

    def y_peer(d):
        return device(z, x, c, lax.rem(y + d, NY))

    def z_peer(d):
        return device(lax.rem(z + d, NZ), x, c, y)

    def x_peer(d):
        return device(z, lax.rem(x + d, NX), c, y)

    sibling = device(z, x, 1 - c, y)

    def send(src, dst, s_sem, r_sem, to):
        copy = pltpu.make_async_remote_copy(
            src_ref=src, dst_ref=dst, send_sem=s_sem, recv_sem=r_sem,
            device_id=to, device_id_type=MESH,
        )
        copy.start()
        return copy

    part = lax.rem(y, 4)
    src_c = y // 4

    def last_source(role, i):
        l = part - role
        at_y = jnp.where(l == 0, z, i)
        at_z = jnp.where(l == 0, i, jnp.where(l == 1, z, 4 * lax.rem(z, 2) + x))
        at_x = jnp.where(l == 2, z // 2, x)
        mine = (at_y == y) & (at_z == z) & (at_x == x) & (src_c == c)
        there = (l >= 0) & (l <= 2)
        return device(at_z, at_x, src_c, at_y), there, mine

    def last_target(l, role, c_to):
        to_y = 4 * c + l + role
        to_z = (y, z, 2 * x + z // 4)[l]
        to_x = (x, x, lax.rem(z, 4))[l]
        mine = (to_y == y) & (to_z == z) & (to_x == x) & (c == c_to)
        return device(to_z, to_x, c_to, to_y), mine

    r3[...] = jnp.zeros_like(r3)

    barrier = pltpu.get_barrier_semaphore()

    def greet(to):
        pl.semaphore_signal(barrier, inc=1, device_id=to, device_id_type=MESH)

    for d in range(1, NY):
        greet(y_peer(d))
    for d in range(1, NZ):
        greet(z_peer(d))
    for d in range(1, NX):
        greet(x_peer(d))
    greet(sibling)
    for role in range(2):

        def hail(i, carry, role=role):
            who, there, mine = last_source(role, i)

            @pl.when(there & jnp.logical_not(mine))
            def _():
                greet(who)

            return carry

        lax.fori_loop(0, NY, hail, 0)
    awaited = (NY - 1) + (NZ - 1) + (NX - 1) + 1
    for l in range(3):
        for role in range(2):
            for c_to in range(2):
                awaited = awaited + jnp.where(last_target(l, role, c_to)[1], 0, 1)

    length = len_ref[0]
    base = y * ROWS
    pick_mask = half(lax.rem(iota((ROWS, D), 0), STEP) == iota((ROWS, D), 1) // HD)
    squeeze = half(iota((PICK, ROWS), 1) // STEP == iota((PICK, ROWS), 0))

    def compact(rows):
        return nn(squeeze, rows * pick_mask).astype(bf16)

    k_sel = compact(k_ref[...])
    v_sel = compact(v_ref[...])
    kv_all[y, 0] = k_sel
    kv_all[y, 1] = v_sel
    gyt[0] = gy_ref[...].T

    pl.semaphore_wait(barrier, awaited)

    kv_copies = [
        send(kv_all.at[y], kv_all.at[y], kv_s.at[d - 1], kv_r.at[d - 1], y_peer(d))
        for d in (1, 7, 2, 6, 3, 5, 4)
    ]
    gyt_copy = send(gyt.at[0], gyt.at[1], core_s.at[0], core_r.at[0], sibling)

    grad[...] = nt(gy_ref[...], w_ref[...]).astype(bf16)
    q_sel = compact(q_ref[...]) * SCALE
    g_sel = compact(grad[...])
    qg_all[y, 0] = q_sel
    qg_all[y, 1] = g_sel
    qg_copies = [
        send(qg_all.at[y], qg_all.at[y], qg_s.at[d - 1], qg_r.at[d - 1], y_peer(d))
        for d in (1, 7, 2, 6, 3, 5, 4)
    ]

    vt[...] = v_ref[...].T
    kt[...] = (k_ref[...] * SCALE).T

    key_ok = base + iota((ROWS, 1), 0) < length
    query_at = iota((1, ROWS), 1)
    query_ok = base + query_at < length

    def pair(p, carry):
        cols = pl.ds(pl.multiple_of(p * 128, 128), 128)
        k2, v2, q2, g2 = k_ref[:, cols], v_ref[:, cols], q_ref[:, cols] * SCALE, grad[:, cols]
        gk2 = jnp.zeros((ROWS, 128), f32)
        gv2 = jnp.zeros((ROWS, 128), f32)
        tops = []
        for e in range(2):
            lanes = half(iota((1, 128), 1) // HD == e)
            own = pl.ds(pl.multiple_of(p * 128 + e * HD, HD), HD)
            q_one, g_one = q2 * lanes, g2 * lanes
            score = jnp.where(key_ok, nt(k2, q_one), NEG)
            ex = jnp.exp(score - jnp.max(score, axis=0, keepdims=True))
            total = jnp.sum(ex, axis=0, keepdims=True)
            used = query_ok & (lax.rem(query_at, STEP) != 2 * p + e)
            prob = ex * jnp.where(used, 1.0 / total, 0.0)
            prob_half = prob.astype(bf16)
            term = prob * nt(v2, g_one)
            dot = jnp.sum(term, axis=0, keepdims=True)
            dscore = (term - prob * dot).astype(bf16)
            tops.append((nn(vt[own, :], prob_half), nn(kt[own, :], dscore)))
            gk2 = gk2 + nn(dscore, q_one)
            gv2 = gv2 + nn(prob_half, g_one)
        att[:, cols] = jnp.concatenate([tops[0][0], tops[1][0]], axis=0).T
        gq_ref[:, cols] = jnp.concatenate([tops[0][1], tops[1][1]], axis=0).T.astype(bf16)
        gk_acc[:, cols] = gk2
        gv_acc[:, cols] = gv2
        return carry

    lax.fori_loop(0, D // 128, pair, 0)

    diagonal = half(iota((COMPACT, D), 0) // PICK == iota((COMPACT, D), 1) // HD)
    spread = half(
        (iota((ROWS, COMPACT), 0) // STEP == lax.rem(iota((ROWS, COMPACT), 1), PICK))
        & (lax.rem(iota((ROWS, COMPACT), 0), STEP) == iota((ROWS, COMPACT), 1) // PICK)
    )

    def block(rows):
        return jnp.concatenate([rows] * HEADS, axis=0) * diagonal

    def place(rows):
        return nn(spread, rows.astype(bf16) * diagonal)

    q_blk = block(q_sel)
    g_blk = block(g_sel)
    row = iota((COMPACT, 1), 0)
    sel_ok = base + lax.rem(row, PICK) * STEP + row // PICK < length
    far_at = (
        iota((COMPACT, FAR), 1) // PICK * ROWS
        + lax.rem(iota((COMPACT, FAR), 1), PICK) * STEP
        + iota((COMPACT, FAR), 0) // PICK
    )
    far_ok = far_at < length
    near_score = jnp.where(query_ok, nt(q_blk, k_ref[...]), NEG)
    near_dprob = nt(g_blk, v_ref[...])

    for copy in kv_copies:
        copy.wait_recv()
    k_far = kv_all[:, 0].reshape(FAR, D)
    v_far = kv_all[:, 1].reshape(FAR, D)

    far_score = jnp.where(far_ok, nt(q_blk, k_far), NEG)
    top = jnp.maximum(
        jnp.max(near_score, axis=1, keepdims=True), jnp.max(far_score, axis=1, keepdims=True)
    )
    near_ex = jnp.exp(near_score - top)
    far_ex = jnp.exp(far_score - top)
    total = jnp.sum(near_ex, axis=1, keepdims=True) + jnp.sum(far_ex, axis=1, keepdims=True)
    inv = jnp.where(sel_ok, 1.0 / total, 0.0)
    near_prob, far_prob = near_ex * inv, far_ex * inv
    near_half, far_half = near_prob.astype(bf16), far_prob.astype(bf16)
    sel_att = nn(near_half, v_ref[...]) + nn(far_half, v_far)
    attended = (att[...] + place(sel_att)).astype(bf16)
    atth[0] = attended[:, : D // 2]
    atth[1] = attended[:, D // 2 :]
    att_copy = send(atth.at[1 - c], att_far, core_s.at[1], core_r.at[1], sibling)

    near_term = near_prob * near_dprob
    far_term = far_prob * nt(g_blk, v_far)
    dot = jnp.sum(near_term, axis=1, keepdims=True) + jnp.sum(far_term, axis=1, keepdims=True)
    lse = jnp.where(sel_ok, top + jnp.log(total), 0.0)
    lane = iota((COMPACT, 128), 1)
    aug = jnp.zeros((COMPACT, 128), f32)
    for at, left in ((0, lse), (3, dot)):
        for n in range(3):
            top_bits = left.astype(bf16).astype(f32)
            aug = jnp.where(lane == (at + n) * STEP + row // PICK, top_bits, aug)
            left = left - top_bits
    aug_all[y] = jnp.sum(aug.reshape(HEADS, PICK, 128), axis=0).astype(bf16)
    aug_copies = [
        send(aug_all.at[y], aug_all.at[y], aug_s.at[d - 1], aug_r.at[d - 1], y_peer(d))
        for d in (1, 7, 2, 6, 3, 5, 4)
    ]

    out_ref[:, : D // 2] = (
        nn(atth[0], w_ref[: D // 2, : D // 2]) + nn(atth[1], w_ref[D // 2 :, : D // 2])
    ).astype(bf16)
    out_ref[:, D // 2 :] = (
        nn(atth[0], w_ref[: D // 2, D // 2 :]) + nn(atth[1], w_ref[D // 2 :, D // 2 :])
    ).astype(bf16)

    gyt_copy.wait_recv()
    att_copy.wait_recv()
    weight = nn(gyt[0], atth[c]) + nn(gyt[1], att_far[...])
    for l in range(3):
        w_full[l] = weight[:, l * 128 : (l + 1) * 128]
    wy[...] = w_full[0].reshape(NY, 96, 128).astype(bf16)
    wz[...] = w_full[1].reshape(NZ, 96, 128).astype(bf16)
    wx[...] = w_full[2].reshape(NX, 192, 128).astype(bf16)
    first = []
    for d in (4, 3, 5, 2, 6, 1, 7):
        first.append(
            send(wy.at[lax.rem(y + d, NY)], r1y.at[d - 1], y_s.at[d - 1], y_r.at[d - 1], y_peer(d))
        )
        first.append(
            send(wz.at[lax.rem(z + d, NZ)], r1z.at[d - 1], z_s.at[d - 1], z_r.at[d - 1], z_peer(d))
        )
        if d < NX:
            first.append(
                send(wx.at[lax.rem(x + d, NX)], r1x.at[d - 1], x_s.at[d - 1], x_r.at[d - 1], x_peer(d))
            )

    near_ds = (near_term - near_prob * dot).astype(bf16)
    far_ds = (far_term - far_prob * dot).astype(bf16)
    sel_gq = (nn(near_ds, k_ref[...]) + nn(far_ds, k_far)) * SCALE
    gq_ref[...] = gq_ref[...] + place(sel_gq).astype(bf16)
    gk_acc[...] += nn(near_ds.astype(f32).T.astype(bf16), q_blk)
    gv_acc[...] += nn(near_prob.T.astype(bf16), g_blk)

    for copy in qg_copies:
        copy.wait_recv()
    for copy in aug_copies:
        copy.wait_recv()
    q_far = qg_all[:, 0].reshape(FAR, D)
    g_far = qg_all[:, 1].reshape(FAR, D)
    aug_far = aug_all[...].reshape(FAR, 128)
    takes = lax.rem(lane, STEP) == row // PICK
    minus_lse = jnp.where(takes & (lane < 3 * STEP), -1.0, 0.0).astype(bf16)
    minus_dot = jnp.where(takes & (lane >= 3 * STEP) & (lane < 6 * STEP), -1.0, 0.0).astype(bf16)
    own_score = nt(block(k_sel), q_far) + nt(minus_lse, aug_far)
    own_prob = jnp.exp(jnp.where(far_ok & sel_ok, own_score, NEG))
    own_ds = own_prob * (nt(block(v_sel), g_far) + nt(minus_dot, aug_far))
    gk_ref[...] = (gk_acc[...] + place(nn(own_ds.astype(bf16), q_far))).astype(bf16)
    gv_ref[...] = (gv_acc[...] + place(nn(own_prob.astype(bf16), g_far))).astype(bf16)

    for copy in first:
        copy.wait_recv()
    sum_y = w_full[0, pl.ds(pl.multiple_of(y * 96, 96), 96)]
    sum_z = w_full[1, pl.ds(pl.multiple_of(z * 96, 96), 96)]
    sum_x = w_full[2, pl.ds(pl.multiple_of(x * 192, 192), 192)]
    for d in range(NY - 1):
        sum_y = sum_y + r1y[d].astype(f32)
        sum_z = sum_z + r1z[d].astype(f32)
    for d in range(NX - 1):
        sum_x = sum_x + r1x[d].astype(f32)
    a0[...] = sum_y.reshape(NX, 24, 128)
    a1[...] = sum_z.reshape(NX, 24, 128)
    a2[...] = sum_x.reshape(NZ, 24, 128)
    second = []
    for d in (4, 3, 5, 2, 6, 1, 7):
        second.append(
            send(a2.at[lax.rem(z + d, NZ)], r22.at[d - 1], b2_s.at[d - 1], b2_r.at[d - 1], z_peer(d))
        )
        if d < NX:
            to = lax.rem(x + d, NX)
            second.append(send(a0.at[to], r20.at[d - 1], b0_s.at[d - 1], b0_r.at[d - 1], x_peer(d)))
            second.append(send(a1.at[to], r21.at[d - 1], b1_s.at[d - 1], b1_r.at[d - 1], x_peer(d)))
    for copy in second:
        copy.wait_recv()
    sums = [a0[x], a1[x], a2[z]]
    for d in range(NX - 1):
        sums[0] = sums[0] + r20[d]
        sums[1] = sums[1] + r21[d]
    for d in range(NZ - 1):
        sums[2] = sums[2] + r22[d]

    from_z = (z, y, y)
    last = []
    for l in range(3):
        s3[l, 0] = sums[l][0:16].astype(bf16)
        s3[l, 1] = sums[l][8:24].astype(bf16)
        for role in range(2):
            for c_to in range(2):
                to, mine = last_target(l, role, c_to)
                n = (l * 2 + role) * 2 + c_to
                copy = pltpu.make_async_remote_copy(
                    src_ref=s3.at[l, c_to], dst_ref=r3.at[role, from_z[l]],
                    send_sem=f_s.at[n], recv_sem=f_r.at[role, from_z[l]],
                    device_id=to, device_id_type=MESH,
                )
                last.append((copy, mine))

                @pl.when(jnp.logical_not(mine))
                def _(copy=copy):
                    copy.start()

                @pl.when(mine)
                def _(l=l, role=role, c_to=c_to):
                    r3[role, from_z[l]] = s3[l, c_to]

    for role in range(2):

        def arrive(i, carry, role=role):
            who, there, mine = last_source(role, i)

            @pl.when(there & jnp.logical_not(mine))
            def _():
                pltpu.make_async_remote_copy(
                    src_ref=s3.at[0, 0], dst_ref=r3.at[role, i],
                    send_sem=f_s.at[0], recv_sem=f_r.at[role, i],
                    device_id=who, device_id_type=MESH,
                ).wait_recv()

            return carry

        lax.fori_loop(0, NY, arrive, 0)

    blocks = [jnp.sum(r3[role].astype(f32), axis=0) for role in (1, 0)]
    turned = jnp.concatenate([blocks[0].T, blocks[1].T], axis=0)
    w_full[0, 0:256, 0:16] = turned
    mine_rows = w_full[0, pl.ds(pl.multiple_of(128 - 32 * part, 32), 96), 0:16]
    wg_ref[...] = jnp.where(c == 0, mine_rows[:, 0:12], mine_rows[:, 4:16])

    for copy in kv_copies + qg_copies + aug_copies + [gyt_copy, att_copy] + first + second:
        copy.wait_send()
    for copy, mine in last:

        @pl.when(jnp.logical_not(mine))
        def _(copy=copy):
            copy.wait_send()


def body(queries, keys, values, grad_y, lengths, w_out):
    vmem = pl.BlockSpec(memory_space=pltpu.VMEM)
    rows = jax.ShapeDtypeStruct((ROWS, D), bf16)
    dma = pltpu.SemaphoreType.DMA
    return pl.pallas_call(
        kernel,
        out_shape=(rows, rows, rows, rows, jax.ShapeDtypeStruct((96, 12), f32)),
        in_specs=[pl.BlockSpec(memory_space=pltpu.SMEM)] + [vmem] * 5,
        out_specs=(vmem,) * 5,
        scratch_shapes=[
            pltpu.VMEM((NY, 2, PICK, D), bf16),
            pltpu.VMEM((NY, 2, PICK, D), bf16),
            pltpu.VMEM((NY, PICK, 128), bf16),
            pltpu.VMEM((2, D, ROWS), bf16),
            pltpu.VMEM((2, ROWS, D // 2), bf16),
            pltpu.VMEM((ROWS, D // 2), bf16),
            pltpu.VMEM((ROWS, D), bf16),
            pltpu.VMEM((ROWS, D), f32),
            pltpu.VMEM((D, ROWS), bf16),
            pltpu.VMEM((D, ROWS), bf16),
            pltpu.VMEM((ROWS, D), f32),
            pltpu.VMEM((ROWS, D), f32),
            pltpu.VMEM((3, D, 128), f32),
            pltpu.VMEM((NY, 96, 128), bf16),
            pltpu.VMEM((NZ, 96, 128), bf16),
            pltpu.VMEM((NX, 192, 128), bf16),
            pltpu.VMEM((NY - 1, 96, 128), bf16),
            pltpu.VMEM((NZ - 1, 96, 128), bf16),
            pltpu.VMEM((NX - 1, 192, 128), bf16),
            pltpu.VMEM((NX, 24, 128), f32),
            pltpu.VMEM((NX, 24, 128), f32),
            pltpu.VMEM((NZ, 24, 128), f32),
            pltpu.VMEM((NX - 1, 24, 128), f32),
            pltpu.VMEM((NX - 1, 24, 128), f32),
            pltpu.VMEM((NZ - 1, 24, 128), f32),
            pltpu.VMEM((3, 2, 16, 128), bf16),
            pltpu.VMEM((2, NY, 16, 128), bf16),
        ]
        + [dma((NY - 1,))] * 6
        + [dma((2,))] * 2
        + [dma((NY - 1,))] * 2
        + [dma((NZ - 1,))] * 2
        + [dma((NX - 1,))] * 2
        + [dma((NX - 1,))] * 4
        + [dma((NZ - 1,))] * 2
        + [dma((12,)), dma((2, NY))],
        compiler_params=pltpu.CompilerParams(
            collective_id=0, has_side_effects=True, vmem_limit_bytes=48 * 1024 * 1024
        ),
    )(lengths, queries, keys, values, grad_y, w_out)


def solution(mesh):
    split = P(("slide", "seq"), None)
    return jax.shard_map(
        body,
        mesh=mesh,
        in_specs=(split, split, split, split, P("slide"), P()),
        out_specs=(split, split, split, split, P("seq", "slide")),
        check_vma=False,
    )
```

```python
import jax
import jax.numpy as jnp
from jax import lax
from jax.experimental import pallas as pl
from jax.experimental.pallas import tpu as pltpu
from jax.sharding import PartitionSpec as P

HEADS = 12
HD = 64
D = 768
ROWS = 256
STEP = 16
PICK = ROWS // STEP
COMPACT = HEADS * PICK
NY, NZ, NX = 8, 8, 4
FAR = NY * PICK
SCALE = HD**-0.5
NEG = -1e30
MESH = pl.DeviceIdType.MESH
bf16 = jnp.bfloat16
f32 = jnp.float32


def nn(a, b):
    return lax.dot_general(a, b, (((1,), (0,)), ((), ())), preferred_element_type=f32)


def nt(a, b):
    return lax.dot_general(a, b, (((1,), (1,)), ((), ())), preferred_element_type=f32)


def iota(shape, dim):
    return lax.broadcasted_iota(jnp.int32, shape, dim)


def half(cond):
    return jnp.where(cond, 1.0, 0.0).astype(bf16)


def kernel(
    len_ref, q_hbm, k_hbm, v_hbm, gy_hbm, w_hbm,
    out_hbm, gq_hbm, gk_hbm, gv_hbm, wg_ref,
    q_ref, k_ref, v_ref, gy_ref, w_ref, out_ref, gq_ref, gk_ref, gv_ref,
    kv_all, qg_all, aug_all, gyt, atth, att_far,
    grad, att, vt, kt, gk_acc, gv_acc,
    w_full, wz, wx, r1z, r1x, sum_x, a1, a2, r21, r22, s3, r3,
    in_s, out_s, kv_s, kv_r, qg_s, qg_r, aug_s, aug_r, core_s, core_r,
    z_s, z_r, x_s, x_r, b1_s, b1_r, b2_s, b2_r, f_s, f_r,
):
    slide = lax.axis_index("slide")
    y = lax.axis_index("seq")
    c = lax.rem(slide, 2)
    x = lax.rem(slide // 2, NX)
    z = slide // (2 * NX)

    def device(z_at, x_at, c_at, y_at):
        return ((z_at * NX + x_at) * 2 + c_at, y_at)

    def y_peer(d):
        return device(z, x, c, lax.rem(y + d, NY))

    def z_peer(d):
        return device(lax.rem(z + d, NZ), x, c, y)

    def x_peer(d):
        return device(z, lax.rem(x + d, NX), c, y)

    sibling = device(z, x, 1 - c, y)

    def send(src, dst, s_sem, r_sem, to):
        copy = pltpu.make_async_remote_copy(
            src_ref=src, dst_ref=dst, send_sem=s_sem, recv_sem=r_sem,
            device_id=to, device_id_type=MESH,
        )
        copy.start()
        return copy

    def load(n, src, dst):
        copy = pltpu.make_async_copy(src, dst, in_s.at[n])
        copy.start()
        return copy

    def store(n, src, dst):
        copy = pltpu.make_async_copy(src, dst, out_s.at[n])
        copy.start()
        return copy

    k_in = load(0, k_hbm, k_ref)
    v_in = load(1, v_hbm, v_ref)
    gy_in = load(2, gy_hbm, gy_ref)
    w_in = load(3, w_hbm, w_ref)
    q_in = load(4, q_hbm, q_ref)

    barrier = pltpu.get_barrier_semaphore()

    def greet(to):
        pl.semaphore_signal(barrier, inc=1, device_id=to, device_id_type=MESH)

    for d in range(1, NY):
        greet(y_peer(d))
    for d in range(1, NZ):
        greet(z_peer(d))
    for d in range(1, NX):
        greet(x_peer(d))
    for d in range(NY):
        greet(device(z, x, 1 - c, lax.rem(y + d, NY)))
    greeted = (NY - 1) + (NZ - 1) + (NX - 1) + NY

    length = len_ref[0]
    base = y * ROWS
    pick_mask = half(lax.rem(iota((ROWS, D), 0), STEP) == iota((ROWS, D), 1) // HD)
    squeeze = half(iota((PICK, ROWS), 1) // STEP == iota((PICK, ROWS), 0))

    def compact(rows):
        return nn(squeeze, rows * pick_mask).astype(bf16)

    k_in.wait()
    k_sel = compact(k_ref[...])
    v_in.wait()
    v_sel = compact(v_ref[...])
    kv_all[y, 0] = k_sel
    kv_all[y, 1] = v_sel

    pl.semaphore_wait(barrier, greeted)

    kv_copies = [
        send(kv_all.at[y], kv_all.at[y], kv_s.at[d - 1], kv_r.at[d - 1], y_peer(d))
        for d in (1, 7, 2, 6, 3, 5, 4)
    ]
    gy_in.wait()
    gyt[0] = gy_ref[...].T
    gyt_copy = send(gyt.at[0], gyt.at[1], core_s.at[0], core_r.at[0], sibling)

    w_in.wait()
    grad[...] = nt(gy_ref[...], w_ref[...]).astype(bf16)
    q_in.wait()
    q_sel = compact(q_ref[...]) * SCALE
    g_sel = compact(grad[...])
    qg_all[y, 0] = q_sel
    qg_all[y, 1] = g_sel
    qg_copies = [
        send(qg_all.at[y], qg_all.at[y], qg_s.at[d - 1], qg_r.at[d - 1], y_peer(d))
        for d in (1, 7, 2, 6, 3, 5, 4)
    ]

    vt[...] = v_ref[...].T
    kt[...] = (k_ref[...] * SCALE).T

    key_ok = base + iota((ROWS, 1), 0) < length
    query_at = iota((1, ROWS), 1)
    query_ok = base + query_at < length

    def pair(p, carry):
        cols = pl.ds(pl.multiple_of(p * 128, 128), 128)
        k2, v2, q2, g2 = k_ref[:, cols], v_ref[:, cols], q_ref[:, cols] * SCALE, grad[:, cols]
        gk2 = jnp.zeros((ROWS, 128), f32)
        gv2 = jnp.zeros((ROWS, 128), f32)
        tops = []
        for e in range(2):
            lanes = half(iota((1, 128), 1) // HD == e)
            own = pl.ds(pl.multiple_of(p * 128 + e * HD, HD), HD)
            q_one, g_one = q2 * lanes, g2 * lanes
            score = jnp.where(key_ok, nt(k2, q_one), NEG)
            ex = jnp.exp(score - jnp.max(score, axis=0, keepdims=True))
            total = jnp.sum(ex, axis=0, keepdims=True)
            used = query_ok & (lax.rem(query_at, STEP) != 2 * p + e)
            prob = ex * jnp.where(used, 1.0 / total, 0.0)
            prob_half = prob.astype(bf16)
            term = prob * nt(v2, g_one)
            dot = jnp.sum(term, axis=0, keepdims=True)
            dscore = (term - prob * dot).astype(bf16)
            tops.append((nn(vt[own, :], prob_half), nn(kt[own, :], dscore)))
            gk2 = gk2 + nn(dscore, q_one)
            gv2 = gv2 + nn(prob_half, g_one)
        att[:, cols] = jnp.concatenate([tops[0][0], tops[1][0]], axis=0).T
        gq_ref[:, cols] = jnp.concatenate([tops[0][1], tops[1][1]], axis=0).T.astype(bf16)
        gk_acc[:, cols] = gk2
        gv_acc[:, cols] = gv2
        return carry

    lax.fori_loop(0, D // 128, pair, 0)

    diagonal = half(iota((COMPACT, D), 0) // PICK == iota((COMPACT, D), 1) // HD)
    spread = half(
        (iota((ROWS, COMPACT), 0) // STEP == lax.rem(iota((ROWS, COMPACT), 1), PICK))
        & (lax.rem(iota((ROWS, COMPACT), 0), STEP) == iota((ROWS, COMPACT), 1) // PICK)
    )

    def block(rows):
        return jnp.concatenate([rows] * HEADS, axis=0) * diagonal

    def place(rows):
        return nn(spread, rows.astype(bf16) * diagonal)

    q_blk = block(q_sel)
    g_blk = block(g_sel)
    row = iota((COMPACT, 1), 0)
    sel_ok = base + lax.rem(row, PICK) * STEP + row // PICK < length
    far_at = (
        iota((COMPACT, FAR), 1) // PICK * ROWS
        + lax.rem(iota((COMPACT, FAR), 1), PICK) * STEP
        + iota((COMPACT, FAR), 0) // PICK
    )
    far_ok = far_at < length
    near_score = jnp.where(query_ok, nt(q_blk, k_ref[...]), NEG)
    near_dprob = nt(g_blk, v_ref[...])

    for copy in kv_copies:
        copy.wait_recv()
    k_far = kv_all[:, 0].reshape(FAR, D)
    v_far = kv_all[:, 1].reshape(FAR, D)

    far_score = jnp.where(far_ok, nt(q_blk, k_far), NEG)
    top = jnp.maximum(
        jnp.max(near_score, axis=1, keepdims=True), jnp.max(far_score, axis=1, keepdims=True)
    )
    near_ex = jnp.exp(near_score - top)
    far_ex = jnp.exp(far_score - top)
    total = jnp.sum(near_ex, axis=1, keepdims=True) + jnp.sum(far_ex, axis=1, keepdims=True)
    inv = jnp.where(sel_ok, 1.0 / total, 0.0)
    near_prob, far_prob = near_ex * inv, far_ex * inv
    near_half, far_half = near_prob.astype(bf16), far_prob.astype(bf16)
    sel_att = nn(near_half, v_ref[...]) + nn(far_half, v_far)
    attended = (att[...] + place(sel_att)).astype(bf16)
    atth[0] = attended[:, : D // 2]
    atth[1] = attended[:, D // 2 :]
    att_copy = send(atth.at[1 - c], att_far, core_s.at[1], core_r.at[1], sibling)

    near_term = near_prob * near_dprob
    far_term = far_prob * nt(g_blk, v_far)
    dot = jnp.sum(near_term, axis=1, keepdims=True) + jnp.sum(far_term, axis=1, keepdims=True)
    lse = jnp.where(sel_ok, top + jnp.log(total), 0.0)
    lane = iota((COMPACT, 128), 1)
    aug = jnp.zeros((COMPACT, 128), f32)
    for at, left in ((0, lse), (3, dot)):
        for n in range(3):
            top_bits = left.astype(bf16).astype(f32)
            aug = jnp.where(lane == (at + n) * STEP + row // PICK, top_bits, aug)
            left = left - top_bits
    aug_all[y] = jnp.sum(aug.reshape(HEADS, PICK, 128), axis=0).astype(bf16)
    aug_copies = [
        send(aug_all.at[y], aug_all.at[y], aug_s.at[d - 1], aug_r.at[d - 1], y_peer(d))
        for d in (1, 7, 2, 6, 3, 5, 4)
    ]

    out_ref[:, : D // 2] = (
        nn(atth[0], w_ref[: D // 2, : D // 2]) + nn(atth[1], w_ref[D // 2 :, : D // 2])
    ).astype(bf16)
    out_ref[:, D // 2 :] = (
        nn(atth[0], w_ref[: D // 2, D // 2 :]) + nn(atth[1], w_ref[D // 2 :, D // 2 :])
    ).astype(bf16)

    stores = [store(0, out_ref, out_hbm)]

    gyt_copy.wait_recv()
    att_copy.wait_recv()
    weight = nn(gyt[0], atth[c]) + nn(gyt[1], att_far[...])
    for l in range(3):
        w_full[l] = weight[:, l * 128 : (l + 1) * 128].reshape(NZ, NX, 24, 128)
    wz[...] = w_full[1].reshape(NZ, 96, 128).astype(bf16)
    for to in range(NX):
        for n, l in enumerate((0, 2)):
            wx[to, n] = w_full[l, :, to].reshape(192, 128).astype(bf16)
    first_x = [
        send(wx.at[lax.rem(x + d, NX)], r1x.at[d - 1], x_s.at[d - 1], x_r.at[d - 1], x_peer(d))
        for d in (2, 1, 3)
    ]
    first_z = [
        send(wz.at[lax.rem(z + d, NZ)], r1z.at[d - 1], z_s.at[d - 1], z_r.at[d - 1], z_peer(d))
        for d in (4, 3, 5, 2, 6, 1, 7)
    ]

    near_ds = (near_term - near_prob * dot).astype(bf16)
    far_ds = (far_term - far_prob * dot).astype(bf16)
    sel_gq = (nn(near_ds, k_ref[...]) + nn(far_ds, k_far)) * SCALE
    gq_ref[...] = gq_ref[...] + place(sel_gq).astype(bf16)
    stores.append(store(1, gq_ref, gq_hbm))
    gk_acc[...] += nn(near_ds.astype(f32).T.astype(bf16), q_blk)
    gv_acc[...] += nn(near_prob.T.astype(bf16), g_blk)

    for copy in qg_copies:
        copy.wait_recv()
    for copy in aug_copies:
        copy.wait_recv()
    q_far = qg_all[:, 0].reshape(FAR, D)
    g_far = qg_all[:, 1].reshape(FAR, D)
    aug_far = aug_all[...].reshape(FAR, 128)
    takes = lax.rem(lane, STEP) == row // PICK
    minus_lse = jnp.where(takes & (lane < 3 * STEP), -1.0, 0.0).astype(bf16)
    minus_dot = jnp.where(takes & (lane >= 3 * STEP) & (lane < 6 * STEP), -1.0, 0.0).astype(bf16)
    own_score = nt(block(k_sel), q_far) + nt(minus_lse, aug_far)
    own_prob = jnp.exp(jnp.where(far_ok & sel_ok, own_score, NEG))
    own_ds = own_prob * (nt(block(v_sel), g_far) + nt(minus_dot, aug_far))
    gk_ref[...] = (gk_acc[...] + place(nn(own_ds.astype(bf16), q_far))).astype(bf16)
    gv_ref[...] = (gv_acc[...] + place(nn(own_prob.astype(bf16), g_far))).astype(bf16)

    stores.append(store(2, gk_ref, gk_hbm))
    stores.append(store(3, gv_ref, gv_hbm))

    for copy in first_x:
        copy.wait_recv()
    for n, l in enumerate((0, 2)):
        block_sum = w_full[l, :, x]
        for d in range(NX - 1):
            block_sum = block_sum + r1x[d, n].astype(f32).reshape(NZ, 24, 128)
        sum_x[n] = block_sum
    a2[...] = jnp.concatenate([sum_x[0], sum_x[1]], axis=1).astype(bf16)
    second_z = [
        send(a2.at[lax.rem(z + d, NZ)], r22.at[d - 1], b2_s.at[d - 1], b2_r.at[d - 1], z_peer(d))
        for d in (4, 3, 5, 2, 6, 1, 7)
    ]
    for copy in first_z:
        copy.wait_recv()
    sum_z = w_full[1, z]
    for d in range(NZ - 1):
        sum_z = sum_z + r1z[d].astype(f32).reshape(NX, 24, 128)
    a1[...] = sum_z
    second_x = [
        send(a1.at[lax.rem(x + d, NX)], r21.at[d - 1], b1_s.at[d - 1], b1_r.at[d - 1], x_peer(d))
        for d in (2, 1, 3)
    ]
    for copy in second_x:
        copy.wait_recv()
    middle = a1[x]
    for d in range(NX - 1):
        middle = middle + r21[d]
    for copy in second_z:
        copy.wait_recv()
    outer = jnp.concatenate([sum_x[0, z], sum_x[1, z]], axis=0)
    for d in range(NZ - 1):
        outer = outer + r22[d].astype(f32)

    zero = jnp.zeros((16, 128), bf16)
    for c_to in range(2):
        s3[c_to, 0] = zero
        s3[c_to, 4] = zero
        for l, rows in enumerate((outer[0:24], middle, outer[24:48])):
            s3[c_to, l + 1] = rows[8 * c_to : 8 * c_to + 16].astype(bf16)
    part = lax.rem(y, 4)
    last = []
    for t in range(4):
        for c_to in range(2):
            mine = (y == 4 * c + t) & (c == c_to)
            copy = pltpu.make_async_remote_copy(
                src_ref=s3.at[c_to, pl.ds(t, 2)], dst_ref=r3.at[y],
                send_sem=f_s.at[2 * t + c_to], recv_sem=f_r.at[y],
                device_id=device(z, x, c_to, 4 * c + t), device_id_type=MESH,
            )
            last.append((copy, mine))

            @pl.when(jnp.logical_not(mine))
            def _(copy=copy):
                copy.start()

            @pl.when(mine)
            def _(t=t, c_to=c_to):
                r3[y] = s3[c_to, pl.ds(t, 2)]

    for at in range(NY):

        @pl.when(jnp.logical_not((y == at) & (c == y // 4)))
        def _(at=at):
            pltpu.make_async_remote_copy(
                src_ref=s3.at[0, pl.ds(0, 2)], dst_ref=r3.at[at],
                send_sem=f_s.at[0], recv_sem=f_r.at[at],
                device_id=device(z, x, y // 4, at), device_id_type=MESH,
            ).wait_recv()

    both = jnp.sum(r3[...].astype(f32), axis=0)
    lanes = jnp.concatenate([both[0], both[1]], axis=1)
    mine_lanes = lanes[:, 128:224]
    for t in range(1, 4):
        mine_lanes = jnp.where(part == t, lanes[:, 128 - 32 * t : 224 - 32 * t], mine_lanes)
    wg_ref[...] = jnp.where(c == 0, mine_lanes[0:12], mine_lanes[4:16])

    sent = kv_copies + qg_copies + aug_copies + [gyt_copy, att_copy]
    for copy in sent + first_x + first_z + second_x + second_z:
        copy.wait_send()
    for copy, mine in last:

        @pl.when(jnp.logical_not(mine))
        def _(copy=copy):
            copy.wait_send()

    for copy in stores:
        copy.wait()


def hand_over(*refs):
    sources, results, held, in_s, out_s = refs[:5], refs[5:10], refs[10:15], refs[15], refs[16]
    loads = [
        pltpu.make_async_copy(src, mid, in_s.at[n])
        for n, (src, mid) in enumerate(zip(sources, held))
    ]
    stores = [
        pltpu.make_async_copy(mid, dst, out_s.at[n])
        for n, (mid, dst) in enumerate(zip(held, results))
    ]
    for copy in loads:
        copy.start()
    for arrived, leaving in zip(loads, stores):
        arrived.wait()
        leaving.start()
    for copy in stores:
        copy.wait()


def body(queries, keys, values, grad_y, lengths, w_out):
    hbm = pl.BlockSpec(memory_space=pltpu.HBM)
    rows = jax.ShapeDtypeStruct((ROWS, D), bf16)
    dma = pltpu.SemaphoreType.DMA
    shapes = (rows, rows, rows, rows, jax.ShapeDtypeStruct((12, 96), f32))
    limit = 60 * 1024 * 1024
    results = pl.pallas_call(
        kernel,
        out_shape=shapes,
        in_specs=[pl.BlockSpec(memory_space=pltpu.SMEM)] + [hbm] * 5,
        out_specs=(hbm,) * 4 + (pl.BlockSpec(memory_space=pltpu.VMEM),),
        scratch_shapes=[
            pltpu.VMEM((ROWS, D), bf16),
            pltpu.VMEM((ROWS, D), bf16),
            pltpu.VMEM((ROWS, D), bf16),
            pltpu.VMEM((ROWS, D), bf16),
            pltpu.VMEM((D, D), bf16),
            pltpu.VMEM((ROWS, D), bf16),
            pltpu.VMEM((ROWS, D), bf16),
            pltpu.VMEM((ROWS, D), bf16),
            pltpu.VMEM((ROWS, D), bf16),
            pltpu.VMEM((NY, 2, PICK, D), bf16),
            pltpu.VMEM((NY, 2, PICK, D), bf16),
            pltpu.VMEM((NY, PICK, 128), bf16),
            pltpu.VMEM((2, D, ROWS), bf16),
            pltpu.VMEM((2, ROWS, D // 2), bf16),
            pltpu.VMEM((ROWS, D // 2), bf16),
            pltpu.VMEM((ROWS, D), bf16),
            pltpu.VMEM((ROWS, D), f32),
            pltpu.VMEM((D, ROWS), bf16),
            pltpu.VMEM((D, ROWS), bf16),
            pltpu.VMEM((ROWS, D), f32),
            pltpu.VMEM((ROWS, D), f32),
            pltpu.VMEM((3, NZ, NX, 24, 128), f32),
            pltpu.VMEM((NZ, 96, 128), bf16),
            pltpu.VMEM((NX, 2, 192, 128), bf16),
            pltpu.VMEM((NZ - 1, 96, 128), bf16),
            pltpu.VMEM((NX - 1, 2, 192, 128), bf16),
            pltpu.VMEM((2, NZ, 24, 128), f32),
            pltpu.VMEM((NX, 24, 128), f32),
            pltpu.VMEM((NZ, 48, 128), bf16),
            pltpu.VMEM((NX - 1, 24, 128), f32),
            pltpu.VMEM((NZ - 1, 48, 128), bf16),
            pltpu.VMEM((2, 5, 16, 128), bf16),
            pltpu.VMEM((NY, 2, 16, 128), bf16),
            dma((5,)),
            dma((4,)),
        ]
        + [dma((NY - 1,))] * 6
        + [dma((2,))] * 2
        + [dma((NZ - 1,))] * 2
        + [dma((NX - 1,))] * 4
        + [dma((NZ - 1,))] * 2
        + [dma((8,)), dma((NY,))],
        compiler_params=pltpu.CompilerParams(
            collective_id=0, has_side_effects=True, vmem_limit_bytes=limit
        ),
    )(lengths, queries, keys, values, grad_y, w_out)
    *grads, weight = pl.pallas_call(
        hand_over,
        out_shape=shapes,
        in_specs=[hbm] * 5,
        out_specs=(hbm,) * 5,
        scratch_shapes=[pltpu.VMEM(shape.shape, shape.dtype) for shape in shapes]
        + [dma((5,)), dma((5,))],
        compiler_params=pltpu.CompilerParams(vmem_limit_bytes=limit),
    )(*results)
    return (*grads, weight.T)


def solution(mesh):
    split = P(("slide", "seq"), None)
    return jax.shard_map(
        body,
        mesh=mesh,
        in_specs=(split, split, split, split, P("slide"), P()),
        out_specs=(split, split, split, split, P("seq", "slide")),
        check_vma=False,
    )
```

```python
import jax
import jax.numpy as jnp
from jax import lax
from jax.experimental import pallas as pl
from jax.experimental.pallas import tpu as pltpu
from jax.sharding import PartitionSpec as P

HD = 64
D = 768
ROWS = 256
STEP = 16
PICK = ROWS // STEP
NY, NZ, NX = 8, 8, 4
FAR = NY * PICK
COMPACT = 4 * PICK
ORDER = (1, 0, 2)
FAR_FIRST = (4, 3, 5, 2, 6, 1, 7)
SCALE = HD**-0.5
NEG = -1e30
MESH = pl.DeviceIdType.MESH
bf16 = jnp.bfloat16
f32 = jnp.float32


def nn(a, b):
    return lax.dot_general(a, b, (((1,), (0,)), ((), ())), preferred_element_type=f32)


def nt(a, b):
    return lax.dot_general(a, b, (((1,), (1,)), ((), ())), preferred_element_type=f32)


def iota(shape, dim):
    return lax.broadcasted_iota(jnp.int32, shape, dim)


def half(cond):
    return jnp.where(cond, 1.0, 0.0).astype(bf16)


def columns(array, l):
    return jnp.concatenate(
        [array[:, 128 * l : 128 * l + 128], array[:, 384 + 128 * l : 512 + 128 * l]], axis=1
    )


def kernel(
    len_ref, q_hbm, k_hbm, v_hbm, gy_hbm, w_hbm,
    out_hbm, gq_hbm, gk_hbm, gv_hbm, wg_ref,
    q_ref, k_ref, v_ref, gy_ref, w_ref, out_ref, gq_ref, gk_ref, gv_ref,
    kv_all, qg_all, aug_all, gyt, atth, att_far,
    grad, att, gk_acc, gv_acc,
    w_full, wz, wx, r1z, r1x, sum_x, a1, a2, r21, r22, s3, r3,
    in_s, out_s, kv_s, kv_r, qg_s, qg_r, aug_s, aug_r, core_s, core_r,
    z_s, z_r, x_s, x_r, b1_s, b1_r, b2_s, b2_r, f_s, f_r,
):
    slide = lax.axis_index("slide")
    y = lax.axis_index("seq")
    c = lax.rem(slide, 2)
    x = lax.rem(slide // 2, NX)
    z = slide // (2 * NX)

    def device(z_at, x_at, c_at, y_at):
        return ((z_at * NX + x_at) * 2 + c_at, y_at)

    def y_peer(d):
        return device(z, x, c, lax.rem(y + d, NY))

    def z_peer(d):
        return device(lax.rem(z + d, NZ), x, c, y)

    def x_peer(d):
        return device(z, lax.rem(x + d, NX), c, y)

    sibling = device(z, x, 1 - c, y)

    def send(src, dst, s_sem, r_sem, to):
        copy = pltpu.make_async_remote_copy(
            src_ref=src, dst_ref=dst, send_sem=s_sem, recv_sem=r_sem,
            device_id=to, device_id_type=MESH,
        )
        copy.start()
        return copy

    def load(n, src, dst):
        copy = pltpu.make_async_copy(src, dst, in_s.at[n])
        copy.start()
        return copy

    def store(n, src, dst):
        copy = pltpu.make_async_copy(src, dst, out_s.at[n])
        copy.start()
        return copy

    k_in = load(0, k_hbm, k_ref)
    v_in = load(1, v_hbm, v_ref)
    gy_in = load(2, gy_hbm, gy_ref)
    w_in = load(3, w_hbm, w_ref)
    q_in = load(4, q_hbm, q_ref)

    barrier = pltpu.get_barrier_semaphore()

    def greet(to):
        pl.semaphore_signal(barrier, inc=1, device_id=to, device_id_type=MESH)

    for d in range(1, NY):
        greet(y_peer(d))
    for d in range(1, NZ):
        greet(z_peer(d))
    for d in range(1, NX):
        greet(x_peer(d))
    for d in range(NY):
        greet(device(z, x, 1 - c, lax.rem(y + d, NY)))
    greeted = (NY - 1) + (NZ - 1) + (NX - 1) + NY

    length = len_ref[0]
    base = y * ROWS
    pick_mask = half(lax.rem(iota((ROWS, D), 0), STEP) == iota((ROWS, D), 1) // HD)
    squeeze = half(iota((PICK, ROWS), 1) // STEP == iota((PICK, ROWS), 0))

    def compact(rows):
        return nn(squeeze, rows * pick_mask).astype(bf16)

    k_in.wait()
    k_sel = compact(k_ref[...])
    v_in.wait()
    v_sel = compact(v_ref[...])
    for l in ORDER:
        kv_all[l, y, 0] = columns(k_sel, l)
        kv_all[l, y, 1] = columns(v_sel, l)

    pl.semaphore_wait(barrier, greeted)

    kv_copies = {}
    for l in ORDER:
        kv_copies[l] = [
            send(
                kv_all.at[l, y], kv_all.at[l, y], kv_s.at[l, d - 1], kv_r.at[l, d - 1], y_peer(d)
            )
            for d in FAR_FIRST
        ]
    gy_in.wait()
    gyt[0] = gy_ref[...].T
    gyt_copy = send(gyt.at[0], gyt.at[1], core_s.at[3], core_r.at[3], sibling)

    w_in.wait()
    grad[...] = nt(gy_ref[...], w_ref[...]).astype(bf16)
    q_in.wait()
    q_sel = compact(q_ref[...]) * SCALE
    g_sel = compact(grad[...])
    qg_all[y, 0] = q_sel
    qg_all[y, 1] = g_sel

    key_ok = base + iota((ROWS, 1), 0) < length
    query_at = iota((1, ROWS), 1)
    query_ok = base + query_at < length

    def dense(l):
        def pair(n, carry):
            p = l + 3 * n
            cols = pl.ds(pl.multiple_of(p * 128, 128), 128)
            k2, v2, q2, g2 = k_ref[:, cols], v_ref[:, cols], q_ref[:, cols] * SCALE, grad[:, cols]
            vt, kt = v2.T, (k2 * SCALE).T
            gk2 = jnp.zeros((ROWS, 128), f32)
            gv2 = jnp.zeros((ROWS, 128), f32)
            tops = []
            for e in range(2):
                lanes = half(iota((1, 128), 1) // HD == e)
                own = slice(e * HD, (e + 1) * HD)
                q_one, g_one = q2 * lanes, g2 * lanes
                score = jnp.where(key_ok, nt(k2, q_one), NEG)
                ex = jnp.exp(score - jnp.max(score, axis=0, keepdims=True))
                total = jnp.sum(ex, axis=0, keepdims=True)
                used = query_ok & (lax.rem(query_at, STEP) != 2 * p + e)
                prob = ex * jnp.where(used, 1.0 / total, 0.0)
                prob_half = prob.astype(bf16)
                term = prob * nt(v2, g_one)
                dot = jnp.sum(term, axis=0, keepdims=True)
                dscore = (term - prob * dot).astype(bf16)
                tops.append((nn(vt[own], prob_half), nn(kt[own], dscore)))
                gk2 = gk2 + nn(dscore, q_one)
                gv2 = gv2 + nn(prob_half, g_one)
            att[:, cols] = jnp.concatenate([tops[0][0], tops[1][0]], axis=0).T
            gq_ref[:, cols] = jnp.concatenate([tops[0][1], tops[1][1]], axis=0).T.astype(bf16)
            gk_acc[:, cols] = gk2
            gv_acc[:, cols] = gv2
            return carry

        lax.fori_loop(0, 2, pair, 0)

    diagonal = half(iota((COMPACT, 256), 0) // PICK == iota((COMPACT, 256), 1) // HD)
    row = iota((COMPACT, 1), 0)
    lane = iota((COMPACT, 128), 1)
    col = iota((ROWS, COMPACT), 1)

    def head_at(l, at):
        return 2 * l + lax.rem(at // PICK, 2) + 6 * (at // (2 * PICK))

    def block(rows):
        return jnp.concatenate([rows] * 4, axis=0) * diagonal

    def spread(l):
        at = iota((ROWS, COMPACT), 0)
        return half((at // STEP == lax.rem(col, PICK)) & (lax.rem(at, STEP) == head_at(l, col)))

    def place(l, rows):
        return nn(spread(l), rows.astype(bf16) * diagonal)

    def oks(l):
        sel_ok = base + lax.rem(row, PICK) * STEP + head_at(l, row) < length
        far_at = lane // PICK * ROWS + lax.rem(lane, PICK) * STEP + head_at(l, row)
        return sel_ok, far_at < length

    def forward(l):
        sel_ok, far_ok = oks(l)
        q_blk, g_blk = block(columns(q_sel, l)), block(columns(g_sel, l))
        k_near, v_near = columns(k_ref, l), columns(v_ref, l)
        near_score = jnp.where(query_ok, nt(q_blk, k_near), NEG)
        near_dprob = nt(g_blk, v_near)
        for copy in kv_copies[l]:
            copy.wait_recv()
        k_far = kv_all[l, :, 0].reshape(FAR, 256)
        v_far = kv_all[l, :, 1].reshape(FAR, 256)
        far_score = jnp.where(far_ok, nt(q_blk, k_far), NEG)
        top = jnp.maximum(
            jnp.max(near_score, axis=1, keepdims=True), jnp.max(far_score, axis=1, keepdims=True)
        )
        near_ex = jnp.exp(near_score - top)
        far_ex = jnp.exp(far_score - top)
        total = jnp.sum(near_ex, axis=1, keepdims=True) + jnp.sum(far_ex, axis=1, keepdims=True)
        inv = jnp.where(sel_ok, 1.0 / total, 0.0)
        near_prob, far_prob = near_ex * inv, far_ex * inv
        sel_att = nn(near_prob.astype(bf16), v_near) + nn(far_prob.astype(bf16), v_far)
        attended = (columns(att, l) + place(l, sel_att)).astype(bf16)
        atth[l, 0] = attended[:, :128]
        atth[l, 1] = attended[:, 128:]
        copy = send(atth.at[l, 1 - c], att_far.at[l], core_s.at[l], core_r.at[l], sibling)
        near_term = near_prob * near_dprob
        far_term = far_prob * nt(g_blk, v_far)
        dot = jnp.sum(near_term, axis=1, keepdims=True) + jnp.sum(far_term, axis=1, keepdims=True)
        aug = jnp.zeros((COMPACT, 128), f32)
        for at, left in ((0, jnp.where(sel_ok, top + jnp.log(total), 0.0)), (3, dot)):
            for n in range(3):
                top_bits = left.astype(bf16).astype(f32)
                aug = jnp.where(lane == (at + n) * STEP + head_at(l, row), top_bits, aug)
                left = left - top_bits
        aug = jnp.sum(aug.reshape(4, PICK, 128), axis=0)
        near_ds = (near_term - near_prob * dot).astype(bf16)
        far_ds = (far_term - far_prob * dot).astype(bf16)
        return copy, attended, aug, (q_blk, g_blk, near_prob, near_ds, far_ds)

    def weight(l, copy):
        copy.wait_recv()
        total = nn(gyt[0], atth[l, c]) + nn(gyt[1], att_far[l])
        w_full[l] = total.reshape(NZ, NX, 24, 128)
        if l == 1:
            wz[...] = total.reshape(NZ, 96, 128).astype(bf16)
            return [
                send(
                    wz.at[lax.rem(z + d, NZ)], r1z.at[d - 1], z_s.at[d - 1], z_r.at[d - 1], z_peer(d)
                )
                for d in FAR_FIRST
            ]
        n = l // 2
        for to in range(NX):
            wx[n, to] = w_full[l, :, to].reshape(192, 128).astype(bf16)
        return [
            send(
                wx.at[n, lax.rem(x + d, NX)], r1x.at[n, d - 1],
                x_s.at[n, d - 1], x_r.at[n, d - 1], x_peer(d),
            )
            for d in (2, 1, 3)
        ]

    dense(1)
    core_1, att_1, aug_1, keep_1 = forward(1)
    dense(0)
    gyt_copy.wait_recv()
    first_z = weight(1, core_1)
    core_0, att_0, aug_0, keep_0 = forward(0)
    dense(2)
    first_0 = weight(0, core_0)
    core_2, att_2, aug_2, keep_2 = forward(2)
    aug_all[y] = (aug_0 + aug_1 + aug_2).astype(bf16)
    qg_copies = [
        send(qg_all.at[y], qg_all.at[y], qg_s.at[d - 1], qg_r.at[d - 1], y_peer(d))
        for d in FAR_FIRST
    ]
    aug_copies = [
        send(aug_all.at[y], aug_all.at[y], aug_s.at[d - 1], aug_r.at[d - 1], y_peer(d))
        for d in FAR_FIRST
    ]
    first_2 = weight(2, core_2)

    def w_rows(l):
        return jnp.concatenate(
            [w_ref[128 * l : 128 * l + 128, :], w_ref[384 + 128 * l : 512 + 128 * l, :]], axis=0
        )

    out_ref[...] = (nn(att_0, w_rows(0)) + nn(att_1, w_rows(1)) + nn(att_2, w_rows(2))).astype(bf16)
    stores = [store(0, out_ref, out_hbm)]

    def put(ref, l, value):
        ref[:, 128 * l : 128 * l + 128] = value[:, :128]
        ref[:, 384 + 128 * l : 512 + 128 * l] = value[:, 128:]

    for l, keep in ((0, keep_0), (1, keep_1), (2, keep_2)):
        q_blk, g_blk, near_prob, near_ds, far_ds = keep
        k_far = kv_all[l, :, 0].reshape(FAR, 256)
        sel_gq = (nn(near_ds, columns(k_ref, l)) + nn(far_ds, k_far)) * SCALE
        put(gq_ref, l, columns(gq_ref, l) + place(l, sel_gq).astype(bf16))
        put(gk_acc, l, columns(gk_acc, l) + nn(near_ds.astype(f32).T.astype(bf16), q_blk))
        put(gv_acc, l, columns(gv_acc, l) + nn(near_prob.T.astype(bf16), g_blk))
    stores.append(store(1, gq_ref, gq_hbm))

    for copy in first_z:
        copy.wait_recv()
    sum_z = w_full[1, z]
    for d in range(NZ - 1):
        sum_z = sum_z + r1z[d].astype(f32).reshape(NX, 24, 128)
    a1[...] = sum_z
    second_x = [
        send(a1.at[lax.rem(x + d, NX)], r21.at[d - 1], b1_s.at[d - 1], b1_r.at[d - 1], x_peer(d))
        for d in (2, 1, 3)
    ]
    second_z = []
    for n, first in enumerate((first_0, first_2)):
        for copy in first:
            copy.wait_recv()
        block_sum = w_full[2 * n, :, x]
        for d in range(NX - 1):
            block_sum = block_sum + r1x[n, d].astype(f32).reshape(NZ, 24, 128)
        sum_x[n] = block_sum
        a2[n] = jnp.concatenate([block_sum, jnp.zeros((NZ, 8, 128), f32)], axis=1).astype(bf16)
        second_z += [
            send(
                a2.at[n, lax.rem(z + d, NZ)], r22.at[n, d - 1],
                b2_s.at[n, d - 1], b2_r.at[n, d - 1], z_peer(d),
            )
            for d in FAR_FIRST
        ]

    for copy in qg_copies:
        copy.wait_recv()
    for copy in aug_copies:
        copy.wait_recv()
    q_far = qg_all[:, 0].reshape(FAR, D)
    g_far = qg_all[:, 1].reshape(FAR, D)
    aug_far = aug_all[...].reshape(FAR, 128)
    for l in range(3):
        sel_ok, far_ok = oks(l)
        takes = lax.rem(lane, STEP) == head_at(l, row)
        minus_lse = jnp.where(takes & (lane < 3 * STEP), -1.0, 0.0).astype(bf16)
        minus_dot = jnp.where(takes & (lane >= 3 * STEP) & (lane < 6 * STEP), -1.0, 0.0).astype(bf16)
        q_l, g_l = columns(q_far, l), columns(g_far, l)
        own_score = nt(block(columns(k_sel, l)), q_l) + nt(minus_lse, aug_far)
        own_prob = jnp.exp(jnp.where(far_ok & sel_ok, own_score, NEG))
        own_ds = own_prob * (nt(block(columns(v_sel, l)), g_l) + nt(minus_dot, aug_far))
        gk_l = columns(gk_acc, l) + place(l, nn(own_ds.astype(bf16), q_l))
        gv_l = columns(gv_acc, l) + place(l, nn(own_prob.astype(bf16), g_l))
        put(gk_ref, l, gk_l.astype(bf16))
        put(gv_ref, l, gv_l.astype(bf16))
    stores.append(store(2, gk_ref, gk_hbm))
    stores.append(store(3, gv_ref, gv_hbm))

    for copy in second_x:
        copy.wait_recv()
    middle = a1[x]
    for d in range(NX - 1):
        middle = middle + r21[d]
    for copy in second_z:
        copy.wait_recv()
    outer = []
    for n in range(2):
        total = sum_x[n, z]
        for d in range(NZ - 1):
            total = total + r22[n, d].astype(f32)[0:24]
        outer.append(total)

    zero = jnp.zeros((16, 128), bf16)
    for c_to in range(2):
        s3[c_to, 0] = zero
        s3[c_to, 4] = zero
        for l, rows in enumerate((outer[0], middle, outer[1])):
            s3[c_to, l + 1] = rows[8 * c_to : 8 * c_to + 16].astype(bf16)
    part = lax.rem(y, 4)
    last = []
    for t in range(4):
        for c_to in range(2):
            mine = (y == 4 * c + t) & (c == c_to)
            copy = pltpu.make_async_remote_copy(
                src_ref=s3.at[c_to, pl.ds(t, 2)], dst_ref=r3.at[y],
                send_sem=f_s.at[2 * t + c_to], recv_sem=f_r.at[y],
                device_id=device(z, x, c_to, 4 * c + t), device_id_type=MESH,
            )
            last.append((copy, mine))

            @pl.when(jnp.logical_not(mine))
            def _(copy=copy):
                copy.start()

            @pl.when(mine)
            def _(t=t, c_to=c_to):
                r3[y] = s3[c_to, pl.ds(t, 2)]

    for at in range(NY):

        @pl.when(jnp.logical_not((y == at) & (c == y // 4)))
        def _(at=at):
            pltpu.make_async_remote_copy(
                src_ref=s3.at[0, pl.ds(0, 2)], dst_ref=r3.at[at],
                send_sem=f_s.at[0], recv_sem=f_r.at[at],
                device_id=device(z, x, y // 4, at), device_id_type=MESH,
            ).wait_recv()

    both = jnp.sum(r3[...].astype(f32), axis=0)
    lanes = jnp.concatenate([both[0], both[1]], axis=1)
    mine_lanes = lanes[:, 128:224]
    for t in range(1, 4):
        mine_lanes = jnp.where(part == t, lanes[:, 128 - 32 * t : 224 - 32 * t], mine_lanes)
    wg_ref[...] = jnp.where(c == 0, mine_lanes[0:12], mine_lanes[4:16])

    sent = kv_copies[0] + kv_copies[1] + kv_copies[2] + qg_copies + aug_copies
    sent += [gyt_copy, core_0, core_1, core_2] + first_z + first_0 + first_2
    for copy in sent + second_x + second_z:
        copy.wait_send()
    for copy, mine in last:

        @pl.when(jnp.logical_not(mine))
        def _(copy=copy):
            copy.wait_send()

    for copy in stores:
        copy.wait()


def hand_over(*refs):
    sources, results, held, in_s, out_s = refs[:5], refs[5:10], refs[10:15], refs[15], refs[16]
    loads = [
        pltpu.make_async_copy(src, mid, in_s.at[n])
        for n, (src, mid) in enumerate(zip(sources, held))
    ]
    stores = [
        pltpu.make_async_copy(mid, dst, out_s.at[n])
        for n, (mid, dst) in enumerate(zip(held, results))
    ]
    for copy in loads:
        copy.start()
    for arrived, leaving in zip(loads, stores):
        arrived.wait()
        leaving.start()
    for copy in stores:
        copy.wait()


def body(queries, keys, values, grad_y, lengths, w_out):
    hbm = pl.BlockSpec(memory_space=pltpu.HBM)
    rows = jax.ShapeDtypeStruct((ROWS, D), bf16)
    dma = pltpu.SemaphoreType.DMA
    shapes = (rows, rows, rows, rows, jax.ShapeDtypeStruct((12, 96), f32))
    limit = 60 * 1024 * 1024
    results = pl.pallas_call(
        kernel,
        out_shape=shapes,
        in_specs=[pl.BlockSpec(memory_space=pltpu.SMEM)] + [hbm] * 5,
        out_specs=(hbm,) * 4 + (pl.BlockSpec(memory_space=pltpu.VMEM),),
        scratch_shapes=[
            pltpu.VMEM((ROWS, D), bf16),
            pltpu.VMEM((ROWS, D), bf16),
            pltpu.VMEM((ROWS, D), bf16),
            pltpu.VMEM((ROWS, D), bf16),
            pltpu.VMEM((D, D), bf16),
            pltpu.VMEM((ROWS, D), bf16),
            pltpu.VMEM((ROWS, D), bf16),
            pltpu.VMEM((ROWS, D), bf16),
            pltpu.VMEM((ROWS, D), bf16),
            pltpu.VMEM((3, NY, 2, PICK, 256), bf16),
            pltpu.VMEM((NY, 2, PICK, D), bf16),
            pltpu.VMEM((NY, PICK, 128), bf16),
            pltpu.VMEM((2, D, ROWS), bf16),
            pltpu.VMEM((3, 2, ROWS, 128), bf16),
            pltpu.VMEM((3, ROWS, 128), bf16),
            pltpu.VMEM((ROWS, D), bf16),
            pltpu.VMEM((ROWS, D), f32),
            pltpu.VMEM((ROWS, D), f32),
            pltpu.VMEM((ROWS, D), f32),
            pltpu.VMEM((3, NZ, NX, 24, 128), f32),
            pltpu.VMEM((NZ, 96, 128), bf16),
            pltpu.VMEM((2, NX, 192, 128), bf16),
            pltpu.VMEM((NZ - 1, 96, 128), bf16),
            pltpu.VMEM((2, NX - 1, 192, 128), bf16),
            pltpu.VMEM((2, NZ, 24, 128), f32),
            pltpu.VMEM((NX, 24, 128), f32),
            pltpu.VMEM((2, NZ, 32, 128), bf16),
            pltpu.VMEM((NX - 1, 24, 128), f32),
            pltpu.VMEM((2, NZ - 1, 32, 128), bf16),
            pltpu.VMEM((2, 5, 16, 128), bf16),
            pltpu.VMEM((NY, 2, 16, 128), bf16),
            dma((5,)),
            dma((4,)),
        ]
        + [dma((3, NY - 1))] * 2
        + [dma((NY - 1,))] * 4
        + [dma((4,))] * 2
        + [dma((NZ - 1,))] * 2
        + [dma((2, NX - 1))] * 2
        + [dma((NX - 1,))] * 2
        + [dma((2, NZ - 1))] * 2
        + [dma((8,)), dma((NY,))],
        compiler_params=pltpu.CompilerParams(
            collective_id=0, has_side_effects=True, vmem_limit_bytes=limit
        ),
    )(lengths, queries, keys, values, grad_y, w_out)
    *grads, weight = pl.pallas_call(
        hand_over,
        out_shape=shapes,
        in_specs=[hbm] * 5,
        out_specs=(hbm,) * 5,
        scratch_shapes=[pltpu.VMEM(shape.shape, shape.dtype) for shape in shapes]
        + [dma((5,)), dma((5,))],
        compiler_params=pltpu.CompilerParams(vmem_limit_bytes=limit),
    )(*results)
    return (*grads, weight.T)


def solution(mesh):
    split = P(("slide", "seq"), None)
    return jax.shard_map(
        body,
        mesh=mesh,
        in_specs=(split, split, split, split, P("slide"), P()),
        out_specs=(split, split, split, split, P("seq", "slide")),
        check_vma=False,
    )
```

```python
import jax
import jax.numpy as jnp
from jax import lax
from jax.experimental import pallas as pl
from jax.experimental.pallas import tpu as pltpu
from jax.sharding import PartitionSpec as P

HD = 64
D = 768
ROWS = 256
STEP = 16
PICK = ROWS // STEP
NY, NZ, NX = 8, 8, 4
FAR = NY * PICK
COMPACT = 4 * PICK
ORDER = (1, 0, 2)
FAR_FIRST = (4, 3, 5, 2, 6, 1, 7)
SCALE = HD**-0.5
NEG = -1e30
MESH = pl.DeviceIdType.MESH
bf16 = jnp.bfloat16
f32 = jnp.float32


def nn(a, b):
    return lax.dot_general(a, b, (((1,), (0,)), ((), ())), preferred_element_type=f32)


def nt(a, b):
    return lax.dot_general(a, b, (((1,), (1,)), ((), ())), preferred_element_type=f32)


def iota(shape, dim):
    return lax.broadcasted_iota(jnp.int32, shape, dim)


def half(cond):
    return jnp.where(cond, 1.0, 0.0).astype(bf16)


def columns(array, l):
    return jnp.concatenate(
        [array[:, 128 * l : 128 * l + 128], array[:, 384 + 128 * l : 512 + 128 * l]], axis=1
    )


def kernel(
    len_ref, q_hbm, k_hbm, v_hbm, gy_hbm, w_hbm,
    out_hbm, gq_hbm, gk_hbm, gv_hbm, wg_ref,
    q_ref, k_ref, v_ref, gy_ref, w_ref, out_ref, gq_ref, gk_ref, gv_ref,
    kv_all, qg_all, aug_all, gyt, atth, att_far,
    grad, att, gk_acc, gv_acc,
    w_full, wz, wx, r1z, r1x, sum_x, a1, a2, r21, r22, s3, r3,
    in_s, out_s, kv_s, kv_r, qg_s, qg_r, aug_s, aug_r, core_s, core_r,
    z_s, z_r, x_s, x_r, b1_s, b1_r, b2_s, b2_r, f_s, f_r,
):
    slide = lax.axis_index("slide")
    y = lax.axis_index("seq")
    c = lax.rem(slide, 2)
    x = lax.rem(slide // 2, NX)
    z = slide // (2 * NX)

    def device(z_at, x_at, c_at, y_at):
        return ((z_at * NX + x_at) * 2 + c_at, y_at)

    def y_peer(d):
        return device(z, x, c, lax.rem(y + d, NY))

    def z_peer(d):
        return device(lax.rem(z + d, NZ), x, c, y)

    def x_peer(d):
        return device(z, lax.rem(x + d, NX), c, y)

    sibling = device(z, x, 1 - c, y)

    def send(src, dst, s_sem, r_sem, to):
        copy = pltpu.make_async_remote_copy(
            src_ref=src, dst_ref=dst, send_sem=s_sem, recv_sem=r_sem,
            device_id=to, device_id_type=MESH,
        )
        copy.start()
        return copy

    def load(n, src, dst):
        copy = pltpu.make_async_copy(src, dst, in_s.at[n])
        copy.start()
        return copy

    def store(n, src, dst):
        copy = pltpu.make_async_copy(src, dst, out_s.at[n])
        copy.start()
        return copy

    barrier = pltpu.get_barrier_semaphore()

    def greet(to):
        pl.semaphore_signal(barrier, inc=1, device_id=to, device_id_type=MESH)

    for d in FAR_FIRST:
        greet(y_peer(d))
    k_in = load(0, k_hbm, k_ref)
    v_in = load(1, v_hbm, v_ref)
    gy_in = load(2, gy_hbm, gy_ref)
    w_in = load(3, w_hbm, w_ref)
    q_in = load(4, q_hbm, q_ref)
    for d in range(1, NZ):
        greet(z_peer(d))
    for d in range(1, NX):
        greet(x_peer(d))
    for d in range(NY):
        greet(device(z, x, 1 - c, lax.rem(y + d, NY)))
    greeted = (NY - 1) + (NZ - 1) + (NX - 1) + NY

    length = len_ref[0]
    base = y * ROWS
    pick_mask = half(lax.rem(iota((ROWS, D), 0), STEP) == iota((ROWS, D), 1) // HD)
    squeeze = half(iota((PICK, ROWS), 1) // STEP == iota((PICK, ROWS), 0))

    def compact(rows):
        return nn(squeeze, rows * pick_mask).astype(bf16)

    k_in.wait()
    k_sel = compact(k_ref[...])
    v_in.wait()
    v_sel = compact(v_ref[...])
    for l in ORDER:
        kv_all[l, y, 0] = columns(k_sel, l)
        kv_all[l, y, 1] = columns(v_sel, l)

    pl.semaphore_wait(barrier, greeted)

    kv_copies = {}
    for l in ORDER:
        kv_copies[l] = [
            send(
                kv_all.at[l, y], kv_all.at[l, y], kv_s.at[l, d - 1], kv_r.at[l, d - 1], y_peer(d)
            )
            for d in FAR_FIRST
        ]
    gy_in.wait()
    gyt[0] = gy_ref[...].T
    gyt_copy = send(gyt.at[0], gyt.at[1], core_s.at[3], core_r.at[3], sibling)

    w_in.wait()
    grad[...] = nt(gy_ref[...], w_ref[...]).astype(bf16)
    q_in.wait()
    q_sel = compact(q_ref[...]) * SCALE
    g_sel = compact(grad[...])
    qg_all[y, 0] = q_sel
    qg_all[y, 1] = g_sel

    key_ok = base + iota((ROWS, 1), 0) < length
    query_at = iota((1, ROWS), 1)
    query_ok = base + query_at < length

    def dense(l):
        def pair(n, carry):
            p = l + 3 * n
            cols = pl.ds(pl.multiple_of(p * 128, 128), 128)
            k2, v2, q2, g2 = k_ref[:, cols], v_ref[:, cols], q_ref[:, cols] * SCALE, grad[:, cols]
            vt, kt = v2.T, (k2 * SCALE).T
            gk2 = jnp.zeros((ROWS, 128), f32)
            gv2 = jnp.zeros((ROWS, 128), f32)
            tops = []
            for e in range(2):
                lanes = half(iota((1, 128), 1) // HD == e)
                own = slice(e * HD, (e + 1) * HD)
                q_one, g_one = q2 * lanes, g2 * lanes
                score = jnp.where(key_ok, nt(k2, q_one), NEG)
                ex = jnp.exp(score - jnp.max(score, axis=0, keepdims=True))
                total = jnp.sum(ex, axis=0, keepdims=True)
                used = query_ok & (lax.rem(query_at, STEP) != 2 * p + e)
                prob = ex * jnp.where(used, 1.0 / total, 0.0)
                prob_half = prob.astype(bf16)
                term = prob * nt(v2, g_one)
                dot = jnp.sum(term, axis=0, keepdims=True)
                dscore = (term - prob * dot).astype(bf16)
                tops.append((nn(vt[own], prob_half), nn(kt[own], dscore)))
                gk2 = gk2 + nn(dscore, q_one)
                gv2 = gv2 + nn(prob_half, g_one)
            att[:, cols] = jnp.concatenate([tops[0][0], tops[1][0]], axis=0).T
            gq_ref[:, cols] = jnp.concatenate([tops[0][1], tops[1][1]], axis=0).T.astype(bf16)
            gk_acc[:, cols] = gk2
            gv_acc[:, cols] = gv2
            return carry

        lax.fori_loop(0, 2, pair, 0)

    diagonal = half(iota((COMPACT, 256), 0) // PICK == iota((COMPACT, 256), 1) // HD)
    row = iota((COMPACT, 1), 0)
    lane = iota((COMPACT, 128), 1)
    col = iota((ROWS, COMPACT), 1)

    def head_at(l, at):
        return 2 * l + lax.rem(at // PICK, 2) + 6 * (at // (2 * PICK))

    def block(rows):
        return jnp.concatenate([rows] * 4, axis=0) * diagonal

    def spread(l):
        at = iota((ROWS, COMPACT), 0)
        return half((at // STEP == lax.rem(col, PICK)) & (lax.rem(at, STEP) == head_at(l, col)))

    def place(l, rows):
        return nn(spread(l), rows.astype(bf16) * diagonal)

    def oks(l):
        sel_ok = base + lax.rem(row, PICK) * STEP + head_at(l, row) < length
        far_at = lane // PICK * ROWS + lax.rem(lane, PICK) * STEP + head_at(l, row)
        return sel_ok, far_at < length

    def forward(l):
        sel_ok, far_ok = oks(l)
        q_blk, g_blk = block(columns(q_sel, l)), block(columns(g_sel, l))
        k_near, v_near = columns(k_ref, l), columns(v_ref, l)
        near_score = jnp.where(query_ok, nt(q_blk, k_near), NEG)
        near_dprob = nt(g_blk, v_near)
        for copy in kv_copies[l]:
            copy.wait_recv()
        k_far = kv_all[l, :, 0].reshape(FAR, 256)
        v_far = kv_all[l, :, 1].reshape(FAR, 256)
        far_score = jnp.where(far_ok, nt(q_blk, k_far), NEG)
        top = jnp.maximum(
            jnp.max(near_score, axis=1, keepdims=True), jnp.max(far_score, axis=1, keepdims=True)
        )
        near_ex = jnp.exp(near_score - top)
        far_ex = jnp.exp(far_score - top)
        total = jnp.sum(near_ex, axis=1, keepdims=True) + jnp.sum(far_ex, axis=1, keepdims=True)
        inv = jnp.where(sel_ok, 1.0 / total, 0.0)
        near_prob, far_prob = near_ex * inv, far_ex * inv
        sel_att = nn(near_prob.astype(bf16), v_near) + nn(far_prob.astype(bf16), v_far)
        attended = (columns(att, l) + place(l, sel_att)).astype(bf16)
        atth[l, 0] = attended[:, :128]
        atth[l, 1] = attended[:, 128:]
        copy = send(atth.at[l, 1 - c], att_far.at[l], core_s.at[l], core_r.at[l], sibling)
        near_term = near_prob * near_dprob
        far_term = far_prob * nt(g_blk, v_far)
        dot = jnp.sum(near_term, axis=1, keepdims=True) + jnp.sum(far_term, axis=1, keepdims=True)
        aug = jnp.zeros((COMPACT, 128), f32)
        for at, left in ((0, jnp.where(sel_ok, top + jnp.log(total), 0.0)), (3, dot)):
            for n in range(3):
                top_bits = left.astype(bf16).astype(f32)
                aug = jnp.where(lane == (at + n) * STEP + head_at(l, row), top_bits, aug)
                left = left - top_bits
        aug = jnp.sum(aug.reshape(4, PICK, 128), axis=0)
        near_ds = (near_term - near_prob * dot).astype(bf16)
        far_ds = (far_term - far_prob * dot).astype(bf16)
        return copy, attended, aug, (q_blk, g_blk, near_prob, near_ds, far_ds)

    def weight(l, copy):
        total = nn(gyt[0], atth[l, c])
        copy.wait_recv()
        total = total + nn(gyt[1], att_far[l])
        w_full[l] = total.reshape(NZ, NX, 24, 128)
        if l == 1:
            wz[...] = total.reshape(NZ, 96, 128).astype(bf16)
            return [
                send(
                    wz.at[lax.rem(z + d, NZ)], r1z.at[d - 1], z_s.at[d - 1], z_r.at[d - 1], z_peer(d)
                )
                for d in FAR_FIRST
            ]
        n = l // 2
        for to in range(NX):
            wx[n, to] = w_full[l, :, to].reshape(192, 128).astype(bf16)
        return [
            send(
                wx.at[n, lax.rem(x + d, NX)], r1x.at[n, d - 1],
                x_s.at[n, d - 1], x_r.at[n, d - 1], x_peer(d),
            )
            for d in (2, 1, 3)
        ]

    for l in ORDER:
        dense(l)
    core_1, att_1, aug_1, keep_1 = forward(1)
    core_0, att_0, aug_0, keep_0 = forward(0)
    gyt_copy.wait_recv()
    first_z = weight(1, core_1)
    core_2, att_2, aug_2, keep_2 = forward(2)
    first_0 = weight(0, core_0)
    aug_all[y] = (aug_0 + aug_1 + aug_2).astype(bf16)
    qg_copies = [
        send(qg_all.at[y], qg_all.at[y], qg_s.at[d - 1], qg_r.at[d - 1], y_peer(d))
        for d in FAR_FIRST
    ]
    aug_copies = [
        send(aug_all.at[y], aug_all.at[y], aug_s.at[d - 1], aug_r.at[d - 1], y_peer(d))
        for d in FAR_FIRST
    ]
    first_2 = weight(2, core_2)

    def w_rows(l):
        return jnp.concatenate(
            [w_ref[128 * l : 128 * l + 128, :], w_ref[384 + 128 * l : 512 + 128 * l, :]], axis=0
        )

    out_ref[...] = (nn(att_0, w_rows(0)) + nn(att_1, w_rows(1)) + nn(att_2, w_rows(2))).astype(bf16)
    stores = [store(0, out_ref, out_hbm)]

    def put(ref, l, value):
        ref[:, 128 * l : 128 * l + 128] = value[:, :128]
        ref[:, 384 + 128 * l : 512 + 128 * l] = value[:, 128:]

    for l, keep in ((0, keep_0), (1, keep_1), (2, keep_2)):
        q_blk, g_blk, near_prob, near_ds, far_ds = keep
        k_far = kv_all[l, :, 0].reshape(FAR, 256)
        sel_gq = (nn(near_ds, columns(k_ref, l)) + nn(far_ds, k_far)) * SCALE
        put(gq_ref, l, columns(gq_ref, l) + place(l, sel_gq).astype(bf16))
        put(gk_acc, l, columns(gk_acc, l) + nn(near_ds.astype(f32).T.astype(bf16), q_blk))
        put(gv_acc, l, columns(gv_acc, l) + nn(near_prob.T.astype(bf16), g_blk))
    stores.append(store(1, gq_ref, gq_hbm))

    for copy in first_z:
        copy.wait_recv()
    sum_z = w_full[1, z]
    for d in range(NZ - 1):
        sum_z = sum_z + r1z[d].astype(f32).reshape(NX, 24, 128)
    a1[...] = sum_z
    second_x = [
        send(a1.at[lax.rem(x + d, NX)], r21.at[d - 1], b1_s.at[d - 1], b1_r.at[d - 1], x_peer(d))
        for d in (2, 1, 3)
    ]
    second_z = []
    for n, first in enumerate((first_0, first_2)):
        for copy in first:
            copy.wait_recv()
        block_sum = w_full[2 * n, :, x]
        for d in range(NX - 1):
            block_sum = block_sum + r1x[n, d].astype(f32).reshape(NZ, 24, 128)
        sum_x[n] = block_sum
        a2[n] = jnp.concatenate([block_sum, jnp.zeros((NZ, 8, 128), f32)], axis=1).astype(bf16)
        second_z.append([
            send(
                a2.at[n, lax.rem(z + d, NZ)], r22.at[n, d - 1],
                b2_s.at[n, d - 1], b2_r.at[n, d - 1], z_peer(d),
            )
            for d in FAR_FIRST
        ])

    for copy in qg_copies:
        copy.wait_recv()
    for copy in aug_copies:
        copy.wait_recv()
    q_far = qg_all[:, 0].reshape(FAR, D)
    g_far = qg_all[:, 1].reshape(FAR, D)
    aug_far = aug_all[...].reshape(FAR, 128)
    for l in range(3):
        sel_ok, far_ok = oks(l)
        takes = lax.rem(lane, STEP) == head_at(l, row)
        minus_lse = jnp.where(takes & (lane < 3 * STEP), -1.0, 0.0).astype(bf16)
        minus_dot = jnp.where(takes & (lane >= 3 * STEP) & (lane < 6 * STEP), -1.0, 0.0).astype(bf16)
        q_l, g_l = columns(q_far, l), columns(g_far, l)
        own_score = nt(block(columns(k_sel, l)), q_l) + nt(minus_lse, aug_far)
        own_prob = jnp.exp(jnp.where(far_ok & sel_ok, own_score, NEG))
        own_ds = own_prob * (nt(block(columns(v_sel, l)), g_l) + nt(minus_dot, aug_far))
        gk_l = columns(gk_acc, l) + place(l, nn(own_ds.astype(bf16), q_l))
        gv_l = columns(gv_acc, l) + place(l, nn(own_prob.astype(bf16), g_l))
        put(gk_ref, l, gk_l.astype(bf16))
        put(gv_ref, l, gv_l.astype(bf16))
    stores.append(store(2, gk_ref, gk_hbm))
    stores.append(store(3, gv_ref, gv_hbm))

    part = lax.rem(y, 4)
    last = []

    def finish(l, total):
        for c_to in range(2):
            s3[l, c_to] = total[8 * c_to : 8 * c_to + 16].astype(bf16)
        for role in range(2):
            for c_to in range(2):
                mine = (y == 4 * c + l + role) & (c == c_to)
                copy = pltpu.make_async_remote_copy(
                    src_ref=s3.at[l, c_to], dst_ref=r3.at[role, y],
                    send_sem=f_s.at[len(last)], recv_sem=f_r.at[role, y],
                    device_id=device(z, x, c_to, 4 * c + l + role), device_id_type=MESH,
                )
                last.append((copy, mine))

                @pl.when(jnp.logical_not(mine))
                def _(copy=copy):
                    copy.start()

                @pl.when(mine)
                def _(l=l, role=role, c_to=c_to):
                    r3[role, y] = s3[l, c_to]

    for copy in second_x:
        copy.wait_recv()
    total = a1[x]
    for d in range(NX - 1):
        total = total + r21[d]
    finish(1, total)
    for n in range(2):
        for copy in second_z[n]:
            copy.wait_recv()
        total = sum_x[n, z]
        for d in range(NZ - 1):
            total = total + r22[n, d].astype(f32)[0:24]
        finish(2 * n, total)

    for role in range(2):

        @pl.when((part < role) | (part > role + 2))
        def _(role=role):
            r3[role] = jnp.zeros((NY, 16, 128), bf16)

        for at in range(NY):

            @pl.when((part >= role) & (part <= role + 2) & jnp.logical_not((y == at) & (c == y // 4)))
            def _(role=role, at=at):
                pltpu.make_async_remote_copy(
                    src_ref=s3.at[0, 0], dst_ref=r3.at[role, at],
                    send_sem=f_s.at[0], recv_sem=f_r.at[role, at],
                    device_id=device(z, x, y // 4, at), device_id_type=MESH,
                ).wait_recv()

    both = jnp.sum(r3[...].astype(f32), axis=1)
    lanes = jnp.concatenate([both[1], both[0]], axis=1)
    mine_lanes = lanes[:, 128:224]
    for t in range(1, 4):
        mine_lanes = jnp.where(part == t, lanes[:, 128 - 32 * t : 224 - 32 * t], mine_lanes)
    wg_ref[...] = jnp.where(c == 0, mine_lanes[0:12], mine_lanes[4:16])

    sent = kv_copies[0] + kv_copies[1] + kv_copies[2] + qg_copies + aug_copies
    sent += [gyt_copy, core_0, core_1, core_2] + first_z + first_0 + first_2
    for copy in sent + second_x + second_z[0] + second_z[1]:
        copy.wait_send()
    for copy, mine in last:

        @pl.when(jnp.logical_not(mine))
        def _(copy=copy):
            copy.wait_send()

    for copy in stores:
        copy.wait()


def hand_over(*refs):
    sources, results, held, in_s, out_s = refs[:5], refs[5:10], refs[10:15], refs[15], refs[16]
    loads = [
        pltpu.make_async_copy(src, mid, in_s.at[n])
        for n, (src, mid) in enumerate(zip(sources, held))
    ]
    stores = [
        pltpu.make_async_copy(mid, dst, out_s.at[n])
        for n, (mid, dst) in enumerate(zip(held, results))
    ]
    for copy in loads:
        copy.start()
    for arrived, leaving in zip(loads, stores):
        arrived.wait()
        leaving.start()
    for copy in stores:
        copy.wait()


def body(queries, keys, values, grad_y, lengths, w_out):
    hbm = pl.BlockSpec(memory_space=pltpu.HBM)
    rows = jax.ShapeDtypeStruct((ROWS, D), bf16)
    dma = pltpu.SemaphoreType.DMA
    shapes = (rows, rows, rows, rows, jax.ShapeDtypeStruct((12, 96), f32))
    limit = 60 * 1024 * 1024
    results = pl.pallas_call(
        kernel,
        out_shape=shapes,
        in_specs=[pl.BlockSpec(memory_space=pltpu.SMEM)] + [hbm] * 5,
        out_specs=(hbm,) * 4 + (pl.BlockSpec(memory_space=pltpu.VMEM),),
        scratch_shapes=[
            pltpu.VMEM((ROWS, D), bf16),
            pltpu.VMEM((ROWS, D), bf16),
            pltpu.VMEM((ROWS, D), bf16),
            pltpu.VMEM((ROWS, D), bf16),
            pltpu.VMEM((D, D), bf16),
            pltpu.VMEM((ROWS, D), bf16),
            pltpu.VMEM((ROWS, D), bf16),
            pltpu.VMEM((ROWS, D), bf16),
            pltpu.VMEM((ROWS, D), bf16),
            pltpu.VMEM((3, NY, 2, PICK, 256), bf16),
            pltpu.VMEM((NY, 2, PICK, D), bf16),
            pltpu.VMEM((NY, PICK, 128), bf16),
            pltpu.VMEM((2, D, ROWS), bf16),
            pltpu.VMEM((3, 2, ROWS, 128), bf16),
            pltpu.VMEM((3, ROWS, 128), bf16),
            pltpu.VMEM((ROWS, D), bf16),
            pltpu.VMEM((ROWS, D), f32),
            pltpu.VMEM((ROWS, D), f32),
            pltpu.VMEM((ROWS, D), f32),
            pltpu.VMEM((3, NZ, NX, 24, 128), f32),
            pltpu.VMEM((NZ, 96, 128), bf16),
            pltpu.VMEM((2, NX, 192, 128), bf16),
            pltpu.VMEM((NZ - 1, 96, 128), bf16),
            pltpu.VMEM((2, NX - 1, 192, 128), bf16),
            pltpu.VMEM((2, NZ, 24, 128), f32),
            pltpu.VMEM((NX, 24, 128), f32),
            pltpu.VMEM((2, NZ, 32, 128), bf16),
            pltpu.VMEM((NX - 1, 24, 128), f32),
            pltpu.VMEM((2, NZ - 1, 32, 128), bf16),
            pltpu.VMEM((3, 2, 16, 128), bf16),
            pltpu.VMEM((2, NY, 16, 128), bf16),
            dma((5,)),
            dma((4,)),
        ]
        + [dma((3, NY - 1))] * 2
        + [dma((NY - 1,))] * 4
        + [dma((4,))] * 2
        + [dma((NZ - 1,))] * 2
        + [dma((2, NX - 1))] * 2
        + [dma((NX - 1,))] * 2
        + [dma((2, NZ - 1))] * 2
        + [dma((12,)), dma((2, NY))],
        compiler_params=pltpu.CompilerParams(
            collective_id=0, has_side_effects=True, vmem_limit_bytes=limit
        ),
    )(lengths, queries, keys, values, grad_y, w_out)
    *grads, weight = pl.pallas_call(
        hand_over,
        out_shape=shapes,
        in_specs=[hbm] * 5,
        out_specs=(hbm,) * 5,
        scratch_shapes=[pltpu.VMEM(shape.shape, shape.dtype) for shape in shapes]
        + [dma((5,)), dma((5,))],
        compiler_params=pltpu.CompilerParams(vmem_limit_bytes=limit),
    )(*results)
    return (*grads, weight.T)


def solution(mesh):
    split = P(("slide", "seq"), None)
    return jax.shard_map(
        body,
        mesh=mesh,
        in_specs=(split, split, split, split, P("slide"), P()),
        out_specs=(split, split, split, split, P("seq", "slide")),
        check_vma=False,
    )
```

```python
import jax
import jax.numpy as jnp
from jax import lax
from jax.experimental import pallas as pl
from jax.experimental.pallas import tpu as pltpu
from jax.sharding import PartitionSpec as P

HD = 64
D = 768
ROWS = 256
STEP = 16
PICK = ROWS // STEP
NY, NZ, NX = 8, 8, 4
FAR = NY * PICK
COMPACT = 4 * PICK
ORDER = (1, 0, 2)
FAR_FIRST = (4, 3, 5, 2, 6, 1, 7)
SCALE = HD**-0.5
NEG = -1e30
MESH = pl.DeviceIdType.MESH
bf16 = jnp.bfloat16
f32 = jnp.float32


def nn(a, b):
    return lax.dot_general(a, b, (((1,), (0,)), ((), ())), preferred_element_type=f32)


def nt(a, b):
    return lax.dot_general(a, b, (((1,), (1,)), ((), ())), preferred_element_type=f32)


def iota(shape, dim):
    return lax.broadcasted_iota(jnp.int32, shape, dim)


def half(cond):
    return jnp.where(cond, 1.0, 0.0).astype(bf16)


def columns(array, l):
    return jnp.concatenate(
        [array[:, 128 * l : 128 * l + 128], array[:, 384 + 128 * l : 512 + 128 * l]], axis=1
    )


def kernel(
    len_ref, q_hbm, k_hbm, v_hbm, gy_hbm, w_hbm,
    out_hbm, gq_hbm, gk_hbm, gv_hbm, wg_ref,
    q_ref, k_ref, v_ref, gy_ref, w_ref, out_ref, gq_ref, gk_ref, gv_ref,
    kv_all, qg_all, aug_all, gyt, atth, att_far,
    grad, att, gk_acc, gv_acc,
    w_full, wz, wx, r1z, r1x, sum_x, a1, a2, r21, r22, s3, r3,
    in_s, out_s, kv_s, kv_r, qg_s, qg_r, aug_s, aug_r, core_s, core_r,
    z_s, z_r, x_s, x_r, b1_s, b1_r, b2_s, b2_r, f_s, f_r,
):
    slide = lax.axis_index("slide")
    y = lax.axis_index("seq")
    c = lax.rem(slide, 2)
    x = lax.rem(slide // 2, NX)
    z = slide // (2 * NX)

    def device(z_at, x_at, c_at, y_at):
        return ((z_at * NX + x_at) * 2 + c_at, y_at)

    def y_peer(d):
        return device(z, x, c, lax.rem(y + d, NY))

    def z_peer(d):
        return device(lax.rem(z + d, NZ), x, c, y)

    def x_peer(d):
        return device(z, lax.rem(x + d, NX), c, y)

    sibling = device(z, x, 1 - c, y)

    def send(src, dst, s_sem, r_sem, to):
        copy = pltpu.make_async_remote_copy(
            src_ref=src, dst_ref=dst, send_sem=s_sem, recv_sem=r_sem,
            device_id=to, device_id_type=MESH,
        )
        copy.start()
        return copy

    def load(n, src, dst):
        copy = pltpu.make_async_copy(src, dst, in_s.at[n])
        copy.start()
        return copy

    def store(n, src, dst):
        copy = pltpu.make_async_copy(src, dst, out_s.at[n])
        copy.start()
        return copy

    barrier = pltpu.get_barrier_semaphore()

    def greet(to):
        pl.semaphore_signal(barrier, inc=1, device_id=to, device_id_type=MESH)

    for d in FAR_FIRST:
        greet(y_peer(d))
    k_in = load(0, k_hbm, k_ref)
    v_in = load(1, v_hbm, v_ref)
    gy_in = load(2, gy_hbm, gy_ref)
    w_in = load(3, w_hbm, w_ref)
    q_in = load(4, q_hbm, q_ref)
    for d in range(1, NZ):
        greet(z_peer(d))
    for d in range(1, NX):
        greet(x_peer(d))
    for d in range(NY):
        greet(device(z, x, 1 - c, lax.rem(y + d, NY)))
    greeted = (NY - 1) + (NZ - 1) + (NX - 1) + NY

    length = len_ref[0]
    base = y * ROWS
    pick_mask = half(lax.rem(iota((ROWS, D), 0), STEP) == iota((ROWS, D), 1) // HD)
    squeeze = half(iota((PICK, ROWS), 1) // STEP == iota((PICK, ROWS), 0))

    def compact(rows):
        return nn(squeeze, rows * pick_mask).astype(bf16)

    k_in.wait()
    k_sel = compact(k_ref[...])
    v_in.wait()
    v_sel = compact(v_ref[...])
    for l in ORDER:
        kv_all[l, y, 0] = columns(k_sel, l)
        kv_all[l, y, 1] = columns(v_sel, l)

    pl.semaphore_wait(barrier, greeted)

    kv_copies = {}
    for l in ORDER:
        kv_copies[l] = [
            send(
                kv_all.at[l, y], kv_all.at[l, y], kv_s.at[l, d - 1], kv_r.at[l, d - 1], y_peer(d)
            )
            for d in FAR_FIRST
        ]
    gy_in.wait()
    gyt[0] = gy_ref[...].T
    gyt_copy = send(gyt.at[0], gyt.at[1], core_s.at[3], core_r.at[3], sibling)

    w_in.wait()
    grad[...] = nt(gy_ref[...], w_ref[...]).astype(bf16)
    q_in.wait()
    q_sel = compact(q_ref[...]) * SCALE
    g_sel = compact(grad[...])
    qg_all[y, 0] = q_sel
    qg_all[y, 1] = g_sel

    key_ok = base + iota((ROWS, 1), 0) < length
    query_at = iota((1, ROWS), 1)
    query_ok = base + query_at < length

    def dense(l):
        def pair(n, carry):
            p = l + 3 * n
            cols = pl.ds(pl.multiple_of(p * 128, 128), 128)
            k2, v2, q2, g2 = k_ref[:, cols], v_ref[:, cols], q_ref[:, cols] * SCALE, grad[:, cols]
            vt, kt = v2.T, (k2 * SCALE).T
            gk2 = jnp.zeros((ROWS, 128), f32)
            gv2 = jnp.zeros((ROWS, 128), f32)
            tops = []
            for e in range(2):
                lanes = half(iota((1, 128), 1) // HD == e)
                own = slice(e * HD, (e + 1) * HD)
                q_one, g_one = q2 * lanes, g2 * lanes
                score = jnp.where(key_ok, nt(k2, q_one), NEG)
                ex = jnp.exp(score - jnp.max(score, axis=0, keepdims=True))
                total = jnp.sum(ex, axis=0, keepdims=True)
                used = query_ok & (lax.rem(query_at, STEP) != 2 * p + e)
                prob = ex * jnp.where(used, 1.0 / total, 0.0)
                prob_half = prob.astype(bf16)
                term = prob * nt(v2, g_one)
                dot = jnp.sum(term, axis=0, keepdims=True)
                dscore = (term - prob * dot).astype(bf16)
                tops.append((nn(vt[own], prob_half), nn(kt[own], dscore)))
                gk2 = gk2 + nn(dscore, q_one)
                gv2 = gv2 + nn(prob_half, g_one)
            att[:, cols] = jnp.concatenate([tops[0][0], tops[1][0]], axis=0).T
            gq_ref[:, cols] = jnp.concatenate([tops[0][1], tops[1][1]], axis=0).T.astype(bf16)
            gk_acc[:, cols] = gk2
            gv_acc[:, cols] = gv2
            return carry

        lax.fori_loop(0, 2, pair, 0)

    diagonal = half(iota((COMPACT, 256), 0) // PICK == iota((COMPACT, 256), 1) // HD)
    row = iota((COMPACT, 1), 0)
    lane = iota((COMPACT, 128), 1)
    col = iota((ROWS, COMPACT), 1)

    def head_at(l, at):
        return 2 * l + lax.rem(at // PICK, 2) + 6 * (at // (2 * PICK))

    def block(rows):
        return jnp.concatenate([rows] * 4, axis=0) * diagonal

    def spread(l):
        at = iota((ROWS, COMPACT), 0)
        return half((at // STEP == lax.rem(col, PICK)) & (lax.rem(at, STEP) == head_at(l, col)))

    def place(l, rows):
        return nn(spread(l), rows.astype(bf16) * diagonal)

    def oks(l):
        sel_ok = base + lax.rem(row, PICK) * STEP + head_at(l, row) < length
        far_at = lane // PICK * ROWS + lax.rem(lane, PICK) * STEP + head_at(l, row)
        return sel_ok, far_at < length

    def forward(l):
        sel_ok, far_ok = oks(l)
        q_blk, g_blk = block(columns(q_sel, l)), block(columns(g_sel, l))
        k_near, v_near = columns(k_ref, l), columns(v_ref, l)
        near_score = jnp.where(query_ok, nt(q_blk, k_near), NEG)
        near_dprob = nt(g_blk, v_near)
        for copy in kv_copies[l]:
            copy.wait_recv()
        k_far = kv_all[l, :, 0].reshape(FAR, 256)
        v_far = kv_all[l, :, 1].reshape(FAR, 256)
        far_score = jnp.where(far_ok, nt(q_blk, k_far), NEG)
        top = jnp.maximum(
            jnp.max(near_score, axis=1, keepdims=True), jnp.max(far_score, axis=1, keepdims=True)
        )
        near_ex = jnp.exp(near_score - top)
        far_ex = jnp.exp(far_score - top)
        total = jnp.sum(near_ex, axis=1, keepdims=True) + jnp.sum(far_ex, axis=1, keepdims=True)
        inv = jnp.where(sel_ok, 1.0 / total, 0.0)
        near_prob, far_prob = near_ex * inv, far_ex * inv
        sel_att = nn(near_prob.astype(bf16), v_near) + nn(far_prob.astype(bf16), v_far)
        attended = (columns(att, l) + place(l, sel_att)).astype(bf16)
        atth[l, 0] = attended[:, :128]
        atth[l, 1] = attended[:, 128:]
        copy = send(atth.at[l, 1 - c], att_far.at[l], core_s.at[l], core_r.at[l], sibling)
        near_term = near_prob * near_dprob
        far_term = far_prob * nt(g_blk, v_far)
        dot = jnp.sum(near_term, axis=1, keepdims=True) + jnp.sum(far_term, axis=1, keepdims=True)
        aug = jnp.zeros((COMPACT, 128), f32)
        for at, left in ((0, jnp.where(sel_ok, top + jnp.log(total), 0.0)), (3, dot)):
            for n in range(3):
                top_bits = left.astype(bf16).astype(f32)
                aug = jnp.where(lane == (at + n) * STEP + head_at(l, row), top_bits, aug)
                left = left - top_bits
        aug = jnp.sum(aug.reshape(4, PICK, 128), axis=0)
        near_ds = (near_term - near_prob * dot).astype(bf16)
        far_ds = (far_term - far_prob * dot).astype(bf16)
        return copy, attended, aug, (q_blk, g_blk, near_prob, near_ds, far_ds)

    def weight(l, copy):
        total = nn(gyt[0], atth[l, c])
        copy.wait_recv()
        total = total + nn(gyt[1], att_far[l])
        w_full[l] = total.reshape(NZ, NX, 24, 128)
        if l == 1:
            wz[...] = total.reshape(NZ, 96, 128).astype(bf16)
            return [
                send(
                    wz.at[lax.rem(z + d, NZ)], r1z.at[d - 1], z_s.at[d - 1], z_r.at[d - 1], z_peer(d)
                )
                for d in FAR_FIRST
            ]
        n = l // 2
        for to in range(NX):
            wx[n, to] = w_full[l, :, to].reshape(192, 128).astype(bf16)
        return [
            send(
                wx.at[n, lax.rem(x + d, NX)], r1x.at[n, d - 1],
                x_s.at[n, d - 1], x_r.at[n, d - 1], x_peer(d),
            )
            for d in (2, 1, 3)
        ]

    for l in ORDER:
        dense(l)
    core_1, att_1, aug_1, keep_1 = forward(1)
    core_0, att_0, aug_0, keep_0 = forward(0)
    gyt_copy.wait_recv()
    first_z = weight(1, core_1)
    core_2, att_2, aug_2, keep_2 = forward(2)
    first_0 = weight(0, core_0)
    aug_all[y] = (aug_0 + aug_1 + aug_2).astype(bf16)
    qg_copies = [
        send(qg_all.at[y], qg_all.at[y], qg_s.at[d - 1], qg_r.at[d - 1], y_peer(d))
        for d in FAR_FIRST
    ]
    aug_copies = [
        send(aug_all.at[y], aug_all.at[y], aug_s.at[d - 1], aug_r.at[d - 1], y_peer(d))
        for d in FAR_FIRST
    ]
    first_2 = weight(2, core_2)

    def put(ref, l, value):
        ref[:, 128 * l : 128 * l + 128] = value[:, :128]
        ref[:, 384 + 128 * l : 512 + 128 * l] = value[:, 128:]

    for l, keep in ((0, keep_0), (1, keep_1), (2, keep_2)):
        q_blk, g_blk, near_prob, near_ds, far_ds = keep
        k_far = kv_all[l, :, 0].reshape(FAR, 256)
        sel_gq = (nn(near_ds, columns(k_ref, l)) + nn(far_ds, k_far)) * SCALE
        put(gq_ref, l, columns(gq_ref, l) + place(l, sel_gq).astype(bf16))
        put(gk_acc, l, columns(gk_acc, l) + nn(near_ds.astype(f32).T.astype(bf16), q_blk))
        put(gv_acc, l, columns(gv_acc, l) + nn(near_prob.T.astype(bf16), g_blk))
    stores = [store(1, gq_ref, gq_hbm)]

    for copy in first_z:
        copy.wait_recv()
    sum_z = w_full[1, z]
    for d in range(NZ - 1):
        sum_z = sum_z + r1z[d].astype(f32).reshape(NX, 24, 128)
    a1[...] = sum_z
    second_x = [
        send(a1.at[lax.rem(x + d, NX)], r21.at[d - 1], b1_s.at[d - 1], b1_r.at[d - 1], x_peer(d))
        for d in (2, 1, 3)
    ]
    second_z = []
    for n, first in enumerate((first_0, first_2)):
        for copy in first:
            copy.wait_recv()
        block_sum = w_full[2 * n, :, x]
        for d in range(NX - 1):
            block_sum = block_sum + r1x[n, d].astype(f32).reshape(NZ, 24, 128)
        sum_x[n] = block_sum
        a2[n] = jnp.concatenate([block_sum, jnp.zeros((NZ, 8, 128), f32)], axis=1).astype(bf16)
        second_z.append([
            send(
                a2.at[n, lax.rem(z + d, NZ)], r22.at[n, d - 1],
                b2_s.at[n, d - 1], b2_r.at[n, d - 1], z_peer(d),
            )
            for d in FAR_FIRST
        ])

    def w_rows(l):
        return jnp.concatenate(
            [w_ref[128 * l : 128 * l + 128, :], w_ref[384 + 128 * l : 512 + 128 * l, :]], axis=0
        )

    out_ref[...] = (nn(att_0, w_rows(0)) + nn(att_1, w_rows(1)) + nn(att_2, w_rows(2))).astype(bf16)
    stores.append(store(0, out_ref, out_hbm))

    part = lax.rem(y, 4)
    last = []

    def finish(l, total):
        for c_to in range(2):
            s3[l, c_to] = total[8 * c_to : 8 * c_to + 16].astype(bf16)
        for role in range(2):
            for c_to in range(2):
                mine = (y == 4 * c + l + role) & (c == c_to)
                copy = pltpu.make_async_remote_copy(
                    src_ref=s3.at[l, c_to], dst_ref=r3.at[role, y],
                    send_sem=f_s.at[len(last)], recv_sem=f_r.at[role, y],
                    device_id=device(z, x, c_to, 4 * c + l + role), device_id_type=MESH,
                )
                last.append((copy, mine))

                @pl.when(jnp.logical_not(mine))
                def _(copy=copy):
                    copy.start()

                @pl.when(mine)
                def _(l=l, role=role, c_to=c_to):
                    r3[role, y] = s3[l, c_to]

    for copy in second_x:
        copy.wait_recv()
    total = a1[x]
    for d in range(NX - 1):
        total = total + r21[d]
    finish(1, total)
    for n in range(2):
        for copy in second_z[n]:
            copy.wait_recv()
        total = sum_x[n, z]
        for d in range(NZ - 1):
            total = total + r22[n, d].astype(f32)[0:24]
        finish(2 * n, total)

    for copy in qg_copies:
        copy.wait_recv()
    for copy in aug_copies:
        copy.wait_recv()
    q_far = qg_all[:, 0].reshape(FAR, D)
    g_far = qg_all[:, 1].reshape(FAR, D)
    aug_far = aug_all[...].reshape(FAR, 128)
    for l in range(3):
        sel_ok, far_ok = oks(l)
        takes = lax.rem(lane, STEP) == head_at(l, row)
        minus_lse = jnp.where(takes & (lane < 3 * STEP), -1.0, 0.0).astype(bf16)
        minus_dot = jnp.where(takes & (lane >= 3 * STEP) & (lane < 6 * STEP), -1.0, 0.0).astype(bf16)
        q_l, g_l = columns(q_far, l), columns(g_far, l)
        own_score = nt(block(columns(k_sel, l)), q_l) + nt(minus_lse, aug_far)
        own_prob = jnp.exp(jnp.where(far_ok & sel_ok, own_score, NEG))
        own_ds = own_prob * (nt(block(columns(v_sel, l)), g_l) + nt(minus_dot, aug_far))
        gk_l = columns(gk_acc, l) + place(l, nn(own_ds.astype(bf16), q_l))
        gv_l = columns(gv_acc, l) + place(l, nn(own_prob.astype(bf16), g_l))
        put(gk_ref, l, gk_l.astype(bf16))
        put(gv_ref, l, gv_l.astype(bf16))
    stores.append(store(2, gk_ref, gk_hbm))
    stores.append(store(3, gv_ref, gv_hbm))

    for role in range(2):

        @pl.when((part < role) | (part > role + 2))
        def _(role=role):
            r3[role] = jnp.zeros((NY, 16, 128), bf16)

        for at in range(NY):

            @pl.when((part >= role) & (part <= role + 2) & jnp.logical_not((y == at) & (c == y // 4)))
            def _(role=role, at=at):
                pltpu.make_async_remote_copy(
                    src_ref=s3.at[0, 0], dst_ref=r3.at[role, at],
                    send_sem=f_s.at[0], recv_sem=f_r.at[role, at],
                    device_id=device(z, x, y // 4, at), device_id_type=MESH,
                ).wait_recv()

    both = jnp.sum(r3[...].astype(f32), axis=1)
    lanes = jnp.concatenate([both[1], both[0]], axis=1)
    mine_lanes = lanes[:, 128:224]
    for t in range(1, 4):
        mine_lanes = jnp.where(part == t, lanes[:, 128 - 32 * t : 224 - 32 * t], mine_lanes)
    wg_ref[...] = jnp.where(c == 0, mine_lanes[0:12], mine_lanes[4:16])

    sent = kv_copies[0] + kv_copies[1] + kv_copies[2] + qg_copies + aug_copies
    sent += [gyt_copy, core_0, core_1, core_2] + first_z + first_0 + first_2
    for copy in sent + second_x + second_z[0] + second_z[1]:
        copy.wait_send()
    for copy, mine in last:

        @pl.when(jnp.logical_not(mine))
        def _(copy=copy):
            copy.wait_send()

    for copy in stores:
        copy.wait()


def hand_over(*refs):
    copies = [
        pltpu.make_async_copy(src, dst, refs[10].at[n])
        for n, (src, dst) in enumerate(zip(refs[:5], refs[5:10]))
    ]
    for copy in copies:
        copy.start()
    for copy in copies:
        copy.wait()


def body(queries, keys, values, grad_y, lengths, w_out):
    hbm = pl.BlockSpec(memory_space=pltpu.HBM)
    anywhere = pl.BlockSpec(memory_space=pl.ANY)
    rows = jax.ShapeDtypeStruct((ROWS, D), bf16)
    dma = pltpu.SemaphoreType.DMA
    shapes = (rows, rows, rows, rows, jax.ShapeDtypeStruct((12, 96), f32))
    limit = 209 * 1024 * 1024 // 4
    results = pl.pallas_call(
        kernel,
        out_shape=shapes,
        in_specs=[pl.BlockSpec(memory_space=pltpu.SMEM)] + [hbm] * 5,
        out_specs=(anywhere,) * 4 + (pl.BlockSpec(memory_space=pltpu.VMEM),),
        scratch_shapes=[
            pltpu.VMEM((ROWS, D), bf16),
            pltpu.VMEM((ROWS, D), bf16),
            pltpu.VMEM((ROWS, D), bf16),
            pltpu.VMEM((ROWS, D), bf16),
            pltpu.VMEM((D, D), bf16),
            pltpu.VMEM((ROWS, D), bf16),
            pltpu.VMEM((ROWS, D), bf16),
            pltpu.VMEM((ROWS, D), bf16),
            pltpu.VMEM((ROWS, D), bf16),
            pltpu.VMEM((3, NY, 2, PICK, 256), bf16),
            pltpu.VMEM((NY, 2, PICK, D), bf16),
            pltpu.VMEM((NY, PICK, 128), bf16),
            pltpu.VMEM((2, D, ROWS), bf16),
            pltpu.VMEM((3, 2, ROWS, 128), bf16),
            pltpu.VMEM((3, ROWS, 128), bf16),
            pltpu.VMEM((ROWS, D), bf16),
            pltpu.VMEM((ROWS, D), f32),
            pltpu.VMEM((ROWS, D), f32),
            pltpu.VMEM((ROWS, D), f32),
            pltpu.VMEM((3, NZ, NX, 24, 128), f32),
            pltpu.VMEM((NZ, 96, 128), bf16),
            pltpu.VMEM((2, NX, 192, 128), bf16),
            pltpu.VMEM((NZ - 1, 96, 128), bf16),
            pltpu.VMEM((2, NX - 1, 192, 128), bf16),
            pltpu.VMEM((2, NZ, 24, 128), f32),
            pltpu.VMEM((NX, 24, 128), f32),
            pltpu.VMEM((2, NZ, 32, 128), bf16),
            pltpu.VMEM((NX - 1, 24, 128), f32),
            pltpu.VMEM((2, NZ - 1, 32, 128), bf16),
            pltpu.VMEM((3, 2, 16, 128), bf16),
            pltpu.VMEM((2, NY, 16, 128), bf16),
            dma((5,)),
            dma((4,)),
        ]
        + [dma((3, NY - 1))] * 2
        + [dma((NY - 1,))] * 4
        + [dma((4,))] * 2
        + [dma((NZ - 1,))] * 2
        + [dma((2, NX - 1))] * 2
        + [dma((NX - 1,))] * 2
        + [dma((2, NZ - 1))] * 2
        + [dma((12,)), dma((2, NY))],
        compiler_params=pltpu.CompilerParams(
            collective_id=0, has_side_effects=True, vmem_limit_bytes=limit
        ),
    )(lengths, queries, keys, values, grad_y, w_out)
    *grads, weight = pl.pallas_call(
        hand_over,
        out_shape=shapes,
        in_specs=[anywhere] * 5,
        out_specs=(hbm,) * 5,
        scratch_shapes=[dma((5,))],
        compiler_params=pltpu.CompilerParams(vmem_limit_bytes=limit),
    )(*results)
    return (*grads, weight.T)


def solution(mesh):
    split = P(("slide", "seq"), None)
    return jax.shard_map(
        body,
        mesh=mesh,
        in_specs=(split, split, split, split, P("slide"), P()),
        out_specs=(split, split, split, split, P("seq", "slide")),
        check_vma=False,
    )
```

```python
import jax
import jax.numpy as jnp
from jax import lax
from jax.experimental import pallas as pl
from jax.experimental.pallas import tpu as pltpu
from jax.sharding import PartitionSpec as P

HD = 64
D = 768
ROWS = 256
STEP = 16
PICK = ROWS // STEP
NY, NZ, NX = 8, 8, 4
FAR = NY * PICK
COMPACT = 4 * PICK
ORDER = (1, 0, 2)
FAR_FIRST = (4, 3, 5, 2, 6, 1, 7)
SCALE = HD**-0.5
NEG = -1e30
MESH = pl.DeviceIdType.MESH
bf16 = jnp.bfloat16
f32 = jnp.float32


def nn(a, b):
    return lax.dot_general(a, b, (((1,), (0,)), ((), ())), preferred_element_type=f32)


def nt(a, b):
    return lax.dot_general(a, b, (((1,), (1,)), ((), ())), preferred_element_type=f32)


def iota(shape, dim):
    return lax.broadcasted_iota(jnp.int32, shape, dim)


def half(cond):
    return jnp.where(cond, 1.0, 0.0).astype(bf16)


def columns(array, l):
    return jnp.concatenate(
        [array[:, 128 * l : 128 * l + 128], array[:, 384 + 128 * l : 512 + 128 * l]], axis=1
    )


def kernel(
    len_ref, q_hbm, k_hbm, v_hbm, gy_hbm, w_hbm,
    out_hbm, gq_hbm, gk_hbm, gv_hbm, wg_ref,
    q_ref, k_ref, v_ref, gy_ref, w_ref, out_ref, gq_ref, gk_ref, gv_ref,
    kv_all, qg_all, aug_all, gyt, atth, att_far,
    grad, att, gk_acc, gv_acc,
    w_full, wz, wx, r1z, r1x, sum_x, a1, a2, r21, r22, s3, r3,
    in_s, out_s, kv_s, kv_r, qg_s, qg_r, aug_s, aug_r, core_s, core_r,
    z_s, z_r, x_s, x_r, b1_s, b1_r, b2_s, b2_r, f_s, f_r,
):
    slide = lax.axis_index("slide")
    y = lax.axis_index("seq")
    c = lax.rem(slide, 2)
    x = lax.rem(slide // 2, NX)
    z = slide // (2 * NX)

    def device(z_at, x_at, c_at, y_at):
        return ((z_at * NX + x_at) * 2 + c_at, y_at)

    def y_peer(d):
        return device(z, x, c, lax.rem(y + d, NY))

    def z_peer(d):
        return device(lax.rem(z + d, NZ), x, c, y)

    def x_peer(d):
        return device(z, lax.rem(x + d, NX), c, y)

    sibling = device(z, x, 1 - c, y)

    def send(src, dst, s_sem, r_sem, to):
        copy = pltpu.make_async_remote_copy(
            src_ref=src, dst_ref=dst, send_sem=s_sem, recv_sem=r_sem,
            device_id=to, device_id_type=MESH,
        )
        copy.start()
        return copy

    def load(n, src, dst):
        copy = pltpu.make_async_copy(src, dst, in_s.at[n])
        copy.start()
        return copy

    def store(n, src, dst):
        copy = pltpu.make_async_copy(src, dst, out_s.at[n])
        copy.start()
        return copy

    barrier = pltpu.get_barrier_semaphore()

    def greet(to):
        pl.semaphore_signal(barrier, inc=1, device_id=to, device_id_type=MESH)

    for d in FAR_FIRST:
        greet(y_peer(d))
        greet(z_peer(d))
        greet(device(z, x, 1 - c, lax.rem(y + d, NY)))
    for d in (2, 1, 3):
        greet(x_peer(d))
    greet(sibling)
    greeted = (NY - 1) + (NZ - 1) + (NX - 1) + NY

    k_in = load(0, k_hbm, k_ref)
    v_in = load(1, v_hbm, v_ref)
    gy_in = load(2, gy_hbm, gy_ref)
    w_in = load(3, w_hbm, w_ref)
    q_in = load(4, q_hbm, q_ref)

    length = len_ref[0]
    base = y * ROWS
    pick_mask = half(lax.rem(iota((ROWS, D), 0), STEP) == iota((ROWS, D), 1) // HD)
    squeeze = half(iota((PICK, ROWS), 1) // STEP == iota((PICK, ROWS), 0))

    def compact(rows):
        return nn(squeeze, rows * pick_mask).astype(bf16)

    k_in.wait()
    k_sel = compact(k_ref[...])
    v_in.wait()
    v_sel = compact(v_ref[...])
    for l in ORDER:
        kv_all[l, y, 0] = columns(k_sel, l)
        kv_all[l, y, 1] = columns(v_sel, l)

    pl.semaphore_wait(barrier, greeted)

    kv_copies = {}
    for l in ORDER:
        kv_copies[l] = [
            send(
                kv_all.at[l, y], kv_all.at[l, y], kv_s.at[l, d - 1], kv_r.at[l, d - 1], y_peer(d)
            )
            for d in FAR_FIRST
        ]
    gy_in.wait()
    gyt[0] = gy_ref[...].T
    gyt_copy = send(gyt.at[0], gyt.at[1], core_s.at[3], core_r.at[3], sibling)

    w_in.wait()
    grad[...] = nt(gy_ref[...], w_ref[...]).astype(bf16)
    q_in.wait()
    q_sel = compact(q_ref[...]) * SCALE
    g_sel = compact(grad[...])
    qg_all[y, 0] = q_sel
    qg_all[y, 1] = g_sel

    key_ok = base + iota((ROWS, 1), 0) < length
    query_at = iota((1, ROWS), 1)
    query_ok = base + query_at < length

    def dense(l):
        def pair(n, carry):
            p = l + 3 * n
            cols = pl.ds(pl.multiple_of(p * 128, 128), 128)
            k2, v2, q2, g2 = k_ref[:, cols], v_ref[:, cols], q_ref[:, cols] * SCALE, grad[:, cols]
            vt, kt = v2.T, (k2 * SCALE).T
            gk2 = jnp.zeros((ROWS, 128), f32)
            gv2 = jnp.zeros((ROWS, 128), f32)
            tops = []
            for e in range(2):
                lanes = half(iota((1, 128), 1) // HD == e)
                own = slice(e * HD, (e + 1) * HD)
                q_one, g_one = q2 * lanes, g2 * lanes
                score = jnp.where(key_ok, nt(k2, q_one), NEG)
                ex = jnp.exp(score - jnp.max(score, axis=0, keepdims=True))
                total = jnp.sum(ex, axis=0, keepdims=True)
                used = query_ok & (lax.rem(query_at, STEP) != 2 * p + e)
                prob = ex * jnp.where(used, 1.0 / total, 0.0)
                prob_half = prob.astype(bf16)
                term = prob * nt(v2, g_one)
                dot = jnp.sum(term, axis=0, keepdims=True)
                dscore = (term - prob * dot).astype(bf16)
                tops.append((nn(vt[own], prob_half), nn(kt[own], dscore)))
                gk2 = gk2 + nn(dscore, q_one)
                gv2 = gv2 + nn(prob_half, g_one)
            att[:, cols] = jnp.concatenate([tops[0][0], tops[1][0]], axis=0).T
            gq_ref[:, cols] = jnp.concatenate([tops[0][1], tops[1][1]], axis=0).T.astype(bf16)
            gk_acc[:, cols] = gk2
            gv_acc[:, cols] = gv2
            return carry

        lax.fori_loop(0, 2, pair, 0)

    diagonal = half(iota((COMPACT, 256), 0) // PICK == iota((COMPACT, 256), 1) // HD)
    row = iota((COMPACT, 1), 0)
    lane = iota((COMPACT, 128), 1)
    col = iota((ROWS, COMPACT), 1)

    def head_at(l, at):
        return 2 * l + lax.rem(at // PICK, 2) + 6 * (at // (2 * PICK))

    def block(rows):
        return jnp.concatenate([rows] * 4, axis=0) * diagonal

    def spread(l):
        at = iota((ROWS, COMPACT), 0)
        return half((at // STEP == lax.rem(col, PICK)) & (lax.rem(at, STEP) == head_at(l, col)))

    def place(l, rows):
        return nn(spread(l), rows.astype(bf16) * diagonal)

    def oks(l):
        sel_ok = base + lax.rem(row, PICK) * STEP + head_at(l, row) < length
        far_at = lane // PICK * ROWS + lax.rem(lane, PICK) * STEP + head_at(l, row)
        return sel_ok, far_at < length

    def forward(l):
        sel_ok, far_ok = oks(l)
        q_blk, g_blk = block(columns(q_sel, l)), block(columns(g_sel, l))
        k_near, v_near = columns(k_ref, l), columns(v_ref, l)
        near_score = jnp.where(query_ok, nt(q_blk, k_near), NEG)
        near_top = jnp.max(near_score, axis=1, keepdims=True)
        near_ex = jnp.exp(near_score - near_top)
        near_total = jnp.sum(near_ex, axis=1, keepdims=True)
        near_att = nn(near_ex.astype(bf16), v_near)
        near_dprob = nt(g_blk, v_near)
        spread_l = spread(l)
        dense_att = columns(att, l)
        for copy in kv_copies[l]:
            copy.wait_recv()
        k_far = kv_all[l, :, 0].reshape(FAR, 256)
        v_far = kv_all[l, :, 1].reshape(FAR, 256)
        far_score = jnp.where(far_ok, nt(q_blk, k_far), NEG)
        top = jnp.maximum(near_top, jnp.max(far_score, axis=1, keepdims=True))
        near_scale = jnp.exp(near_top - top)
        far_ex = jnp.exp(far_score - top)
        total = near_total * near_scale + jnp.sum(far_ex, axis=1, keepdims=True)
        inv = jnp.where(sel_ok, 1.0 / total, 0.0)
        near_inv = near_scale * inv
        sel_att = near_att * near_inv + nn(far_ex.astype(bf16), v_far) * inv
        attended = (dense_att + nn(spread_l, sel_att.astype(bf16) * diagonal)).astype(bf16)
        atth[l, 0] = attended[:, :128]
        atth[l, 1] = attended[:, 128:]
        copy = send(atth.at[l, 1 - c], att_far.at[l], core_s.at[l], core_r.at[l], sibling)
        near_prob, far_prob = near_ex * near_inv, far_ex * inv
        near_term = near_prob * near_dprob
        far_term = far_prob * nt(g_blk, v_far)
        dot = jnp.sum(near_term, axis=1, keepdims=True) + jnp.sum(far_term, axis=1, keepdims=True)
        aug = jnp.zeros((COMPACT, 128), f32)
        for at, left in ((0, jnp.where(sel_ok, top + jnp.log(total), 0.0)), (3, dot)):
            for n in range(3):
                top_bits = left.astype(bf16).astype(f32)
                aug = jnp.where(lane == (at + n) * STEP + head_at(l, row), top_bits, aug)
                left = left - top_bits
        aug = jnp.sum(aug.reshape(4, PICK, 128), axis=0)
        near_ds = (near_term - near_prob * dot).astype(bf16)
        far_ds = (far_term - far_prob * dot).astype(bf16)
        return copy, attended, aug, (q_blk, g_blk, near_prob, near_ds, far_ds)

    def weight(l, copy):
        total = nn(gyt[0], atth[l, c])
        copy.wait_recv()
        total = total + nn(gyt[1], att_far[l])
        w_full[l] = total.reshape(NZ, NX, 24, 128)
        if l == 1:
            wz[...] = total.reshape(NZ, 96, 128).astype(bf16)
            return [
                send(
                    wz.at[lax.rem(z + d, NZ)], r1z.at[d - 1], z_s.at[d - 1], z_r.at[d - 1], z_peer(d)
                )
                for d in FAR_FIRST
            ]
        n = l // 2
        copies = []
        for d in (2, 1, 3):
            to = lax.rem(x + d, NX)
            wx[n, to] = w_full[l, :, to].reshape(192, 128).astype(bf16)
            copies.append(
                send(wx.at[n, to], r1x.at[n, d - 1], x_s.at[n, d - 1], x_r.at[n, d - 1], x_peer(d))
            )
        return copies

    for l in ORDER:
        dense(l)
    core_1, att_1, aug_1, keep_1 = forward(1)
    core_0, att_0, aug_0, keep_0 = forward(0)
    gyt_copy.wait_recv()
    first_z = weight(1, core_1)
    core_2, att_2, aug_2, keep_2 = forward(2)
    first_0 = weight(0, core_0)
    aug_all[y] = (aug_0 + aug_1 + aug_2).astype(bf16)
    qg_copies = [
        send(qg_all.at[y], qg_all.at[y], qg_s.at[d - 1], qg_r.at[d - 1], y_peer(d))
        for d in FAR_FIRST
    ]
    aug_copies = [
        send(aug_all.at[y], aug_all.at[y], aug_s.at[d - 1], aug_r.at[d - 1], y_peer(d))
        for d in FAR_FIRST
    ]
    first_2 = weight(2, core_2)

    def put(ref, l, value):
        ref[:, 128 * l : 128 * l + 128] = value[:, :128]
        ref[:, 384 + 128 * l : 512 + 128 * l] = value[:, 128:]

    for l, keep in ((0, keep_0), (1, keep_1), (2, keep_2)):
        q_blk, g_blk, near_prob, near_ds, far_ds = keep
        k_far = kv_all[l, :, 0].reshape(FAR, 256)
        sel_gq = (nn(near_ds, columns(k_ref, l)) + nn(far_ds, k_far)) * SCALE
        put(gq_ref, l, columns(gq_ref, l) + place(l, sel_gq).astype(bf16))
        put(gk_acc, l, columns(gk_acc, l) + nn(near_ds.astype(f32).T.astype(bf16), q_blk))
        put(gv_acc, l, columns(gv_acc, l) + nn(near_prob.T.astype(bf16), g_blk))
    stores = [store(1, gq_ref, gq_hbm)]

    for copy in first_z:
        copy.wait_recv()
    sum_z = w_full[1, z]
    for d in range(NZ - 1):
        sum_z = sum_z + r1z[d].astype(f32).reshape(NX, 24, 128)
    a1[...] = sum_z
    second_x = [
        send(a1.at[lax.rem(x + d, NX)], r21.at[d - 1], b1_s.at[d - 1], b1_r.at[d - 1], x_peer(d))
        for d in (2, 1, 3)
    ]
    second_z = []
    for n, first in enumerate((first_0, first_2)):
        for copy in first:
            copy.wait_recv()
        block_sum = w_full[2 * n, :, x]
        for d in range(NX - 1):
            block_sum = block_sum + r1x[n, d].astype(f32).reshape(NZ, 24, 128)
        sum_x[n] = block_sum
        a2[n] = jnp.concatenate([block_sum, jnp.zeros((NZ, 8, 128), f32)], axis=1).astype(bf16)
        second_z.append([
            send(
                a2.at[n, lax.rem(z + d, NZ)], r22.at[n, d - 1],
                b2_s.at[n, d - 1], b2_r.at[n, d - 1], z_peer(d),
            )
            for d in FAR_FIRST
        ])

    def w_rows(l):
        return jnp.concatenate(
            [w_ref[128 * l : 128 * l + 128, :], w_ref[384 + 128 * l : 512 + 128 * l, :]], axis=0
        )

    out_ref[...] = (nn(att_0, w_rows(0)) + nn(att_1, w_rows(1)) + nn(att_2, w_rows(2))).astype(bf16)
    stores.append(store(0, out_ref, out_hbm))

    part = lax.rem(y, 4)
    last = []

    def finish(l, total):
        for c_to in range(2):
            s3[l, c_to] = total[8 * c_to : 8 * c_to + 16].astype(bf16)
        for role in range(2):
            for c_to in range(2):
                mine = (y == 4 * c + l + role) & (c == c_to)
                copy = pltpu.make_async_remote_copy(
                    src_ref=s3.at[l, c_to], dst_ref=r3.at[role, y],
                    send_sem=f_s.at[len(last)], recv_sem=f_r.at[role, y],
                    device_id=device(z, x, c_to, 4 * c + l + role), device_id_type=MESH,
                )
                last.append((copy, mine))

                @pl.when(jnp.logical_not(mine))
                def _(copy=copy):
                    copy.start()

                @pl.when(mine)
                def _(l=l, role=role, c_to=c_to):
                    r3[role, y] = s3[l, c_to]

    for copy in second_x:
        copy.wait_recv()
    total = a1[x]
    for d in range(NX - 1):
        total = total + r21[d]
    finish(1, total)
    for n in range(2):
        for copy in second_z[n]:
            copy.wait_recv()
        total = sum_x[n, z]
        for d in range(NZ - 1):
            total = total + r22[n, d].astype(f32)[0:24]
        finish(2 * n, total)

    for copy in qg_copies:
        copy.wait_recv()
    for copy in aug_copies:
        copy.wait_recv()
    q_far = qg_all[:, 0].reshape(FAR, D)
    g_far = qg_all[:, 1].reshape(FAR, D)
    aug_far = aug_all[...].reshape(FAR, 128)
    for l in range(3):
        sel_ok, far_ok = oks(l)
        takes = lax.rem(lane, STEP) == head_at(l, row)
        minus_lse = jnp.where(takes & (lane < 3 * STEP), -1.0, 0.0).astype(bf16)
        minus_dot = jnp.where(takes & (lane >= 3 * STEP) & (lane < 6 * STEP), -1.0, 0.0).astype(bf16)
        q_l, g_l = columns(q_far, l), columns(g_far, l)
        own_score = nt(block(columns(k_sel, l)), q_l) + nt(minus_lse, aug_far)
        own_prob = jnp.exp(jnp.where(far_ok & sel_ok, own_score, NEG))
        own_ds = own_prob * (nt(block(columns(v_sel, l)), g_l) + nt(minus_dot, aug_far))
        gk_l = columns(gk_acc, l) + place(l, nn(own_ds.astype(bf16), q_l))
        gv_l = columns(gv_acc, l) + place(l, nn(own_prob.astype(bf16), g_l))
        put(gk_ref, l, gk_l.astype(bf16))
        put(gv_ref, l, gv_l.astype(bf16))
    stores.append(store(2, gk_ref, gk_hbm))
    stores.append(store(3, gv_ref, gv_hbm))

    sent = kv_copies[0] + kv_copies[1] + kv_copies[2] + qg_copies + aug_copies
    sent += [gyt_copy, core_0, core_1, core_2] + first_z + first_0 + first_2
    for copy in sent + second_x + second_z[0] + second_z[1]:
        copy.wait_send()
    for copy in stores:
        copy.wait()

    for copy, mine in last:

        @pl.when(jnp.logical_not(mine))
        def _(copy=copy):
            copy.wait_send()

    for role in range(2):

        @pl.when((part < role) | (part > role + 2))
        def _(role=role):
            r3[role] = jnp.zeros((NY, 16, 128), bf16)

        for at in range(NY):

            @pl.when((part >= role) & (part <= role + 2) & jnp.logical_not((y == at) & (c == y // 4)))
            def _(role=role, at=at):
                pltpu.make_async_remote_copy(
                    src_ref=s3.at[0, 0], dst_ref=r3.at[role, at],
                    send_sem=f_s.at[0], recv_sem=f_r.at[role, at],
                    device_id=device(z, x, y // 4, at), device_id_type=MESH,
                ).wait_recv()

    both = jnp.sum(r3[...].astype(f32), axis=1)
    lanes = jnp.concatenate([both[1], both[0]], axis=1)
    mine_lanes = lanes[:, 128:224]
    for t in range(1, 4):
        mine_lanes = jnp.where(part == t, lanes[:, 128 - 32 * t : 224 - 32 * t], mine_lanes)
    wg_ref[...] = jnp.where(c == 0, mine_lanes[0:12], mine_lanes[4:16])


def hand_over(*refs):
    copies = [
        pltpu.make_async_copy(src, dst, refs[10].at[n])
        for n, (src, dst) in enumerate(zip(refs[:5], refs[5:10]))
    ]
    for copy in copies:
        copy.start()
    for copy in copies:
        copy.wait()


def body(queries, keys, values, grad_y, lengths, w_out):
    hbm = pl.BlockSpec(memory_space=pltpu.HBM)
    anywhere = pl.BlockSpec(memory_space=pl.ANY)
    rows = jax.ShapeDtypeStruct((ROWS, D), bf16)
    dma = pltpu.SemaphoreType.DMA
    shapes = (rows, rows, rows, rows, jax.ShapeDtypeStruct((12, 96), f32))
    limit = 209 * 1024 * 1024 // 4
    results = pl.pallas_call(
        kernel,
        out_shape=shapes,
        in_specs=[pl.BlockSpec(memory_space=pltpu.SMEM)] + [hbm] * 5,
        out_specs=(anywhere,) * 4 + (pl.BlockSpec(memory_space=pltpu.VMEM),),
        scratch_shapes=[
            pltpu.VMEM((ROWS, D), bf16),
            pltpu.VMEM((ROWS, D), bf16),
            pltpu.VMEM((ROWS, D), bf16),
            pltpu.VMEM((ROWS, D), bf16),
            pltpu.VMEM((D, D), bf16),
            pltpu.VMEM((ROWS, D), bf16),
            pltpu.VMEM((ROWS, D), bf16),
            pltpu.VMEM((ROWS, D), bf16),
            pltpu.VMEM((ROWS, D), bf16),
            pltpu.VMEM((3, NY, 2, PICK, 256), bf16),
            pltpu.VMEM((NY, 2, PICK, D), bf16),
            pltpu.VMEM((NY, PICK, 128), bf16),
            pltpu.VMEM((2, D, ROWS), bf16),
            pltpu.VMEM((3, 2, ROWS, 128), bf16),
            pltpu.VMEM((3, ROWS, 128), bf16),
            pltpu.VMEM((ROWS, D), bf16),
            pltpu.VMEM((ROWS, D), f32),
            pltpu.VMEM((ROWS, D), f32),
            pltpu.VMEM((ROWS, D), f32),
            pltpu.VMEM((3, NZ, NX, 24, 128), f32),
            pltpu.VMEM((NZ, 96, 128), bf16),
            pltpu.VMEM((2, NX, 192, 128), bf16),
            pltpu.VMEM((NZ - 1, 96, 128), bf16),
            pltpu.VMEM((2, NX - 1, 192, 128), bf16),
            pltpu.VMEM((2, NZ, 24, 128), f32),
            pltpu.VMEM((NX, 24, 128), f32),
            pltpu.VMEM((2, NZ, 32, 128), bf16),
            pltpu.VMEM((NX - 1, 24, 128), f32),
            pltpu.VMEM((2, NZ - 1, 32, 128), bf16),
            pltpu.VMEM((3, 2, 16, 128), bf16),
            pltpu.VMEM((2, NY, 16, 128), bf16),
            dma((5,)),
            dma((4,)),
        ]
        + [dma((3, NY - 1))] * 2
        + [dma((NY - 1,))] * 4
        + [dma((4,))] * 2
        + [dma((NZ - 1,))] * 2
        + [dma((2, NX - 1))] * 2
        + [dma((NX - 1,))] * 2
        + [dma((2, NZ - 1))] * 2
        + [dma((12,)), dma((2, NY))],
        compiler_params=pltpu.CompilerParams(
            collective_id=0, has_side_effects=True, vmem_limit_bytes=limit
        ),
    )(lengths, queries, keys, values, grad_y, w_out)
    *grads, weight = pl.pallas_call(
        hand_over,
        out_shape=shapes,
        in_specs=[anywhere] * 5,
        out_specs=(hbm,) * 5,
        scratch_shapes=[dma((5,))],
        compiler_params=pltpu.CompilerParams(vmem_limit_bytes=limit),
    )(*results)
    return (*grads, weight.T)


def solution(mesh):
    split = P(("slide", "seq"), None)
    return jax.shard_map(
        body,
        mesh=mesh,
        in_specs=(split, split, split, split, P("slide"), P()),
        out_specs=(split, split, split, split, P("seq", "slide")),
        check_vma=False,
    )
```

```python
import jax
import jax.numpy as jnp
from jax import lax
from jax.experimental import pallas as pl
from jax.experimental.pallas import tpu as pltpu
from jax.sharding import PartitionSpec as P

HD = 64
D = 768
ROWS = 256
STEP = 16
PICK = ROWS // STEP
NY, NZ, NX = 8, 8, 4
FAR = NY * PICK
COMPACT = 4 * PICK
ORDER = (0, 1, 2)
FAR_FIRST = (4, 3, 5, 2, 6, 1, 7)
SCALE = HD**-0.5
NEG = -1e30
MESH = pl.DeviceIdType.MESH
bf16 = jnp.bfloat16
f32 = jnp.float32


def nn(a, b):
    return lax.dot_general(a, b, (((1,), (0,)), ((), ())), preferred_element_type=f32)


def nt(a, b):
    return lax.dot_general(a, b, (((1,), (1,)), ((), ())), preferred_element_type=f32)


def iota(shape, dim):
    return lax.broadcasted_iota(jnp.int32, shape, dim)


def half(cond):
    return jnp.where(cond, 1.0, 0.0).astype(bf16)


def columns(array, l):
    return jnp.concatenate(
        [array[:, 128 * l : 128 * l + 128], array[:, 384 + 128 * l : 512 + 128 * l]], axis=1
    )


def kernel(
    len_ref, q_hbm, k_hbm, v_hbm, gy_hbm, w_hbm,
    out_hbm, gq_hbm, gk_hbm, gv_hbm, wg_ref,
    q_ref, k_ref, v_ref, gy_ref, w_ref, out_ref, gq_ref, gk_ref, gv_ref,
    kv_all, qg_all, aug_all, gyt, atth, att_far,
    grad, att, gk_acc, gv_acc,
    w_full, wz, wx, r1z, r1x, sum_x, a1, a2, r21, r22, s3, r3,
    in_s, out_s, kv_s, kv_r, qg_s, qg_r, aug_s, aug_r, core_s, core_r,
    z_s, z_r, x_s, x_r, b1_s, b1_r, b2_s, b2_r, f_s, f_r,
):
    slide = lax.axis_index("slide")
    y = lax.axis_index("seq")
    c = lax.rem(slide, 2)
    x = lax.rem(slide // 2, NX)
    z = slide // (2 * NX)

    def device(z_at, x_at, c_at, y_at):
        return ((z_at * NX + x_at) * 2 + c_at, y_at)

    def y_peer(d):
        return device(z, x, c, lax.rem(y + d, NY))

    def z_peer(d):
        return device(lax.rem(z + d, NZ), x, c, y)

    def x_peer(d):
        return device(z, lax.rem(x + d, NX), c, y)

    sibling = device(z, x, 1 - c, y)

    def send(src, dst, s_sem, r_sem, to):
        copy = pltpu.make_async_remote_copy(
            src_ref=src, dst_ref=dst, send_sem=s_sem, recv_sem=r_sem,
            device_id=to, device_id_type=MESH,
        )
        copy.start()
        return copy

    def load(n, src, dst):
        copy = pltpu.make_async_copy(src, dst, in_s.at[n])
        copy.start()
        return copy

    def store(n, src, dst):
        copy = pltpu.make_async_copy(src, dst, out_s.at[n])
        copy.start()
        return copy

    barrier = pltpu.get_barrier_semaphore()

    def greet(to):
        pl.semaphore_signal(barrier, inc=1, device_id=to, device_id_type=MESH)

    for d in FAR_FIRST:
        greet(y_peer(d))
        greet(z_peer(d))
        greet(device(z, x, 1 - c, lax.rem(y + d, NY)))
    for d in (2, 1, 3):
        greet(x_peer(d))
    greet(sibling)
    greeted = (NY - 1) + (NZ - 1) + (NX - 1) + NY

    k_in = load(0, k_hbm, k_ref)
    v_in = load(1, v_hbm, v_ref)
    gy_in = load(2, gy_hbm, gy_ref)
    w_in = load(3, w_hbm, w_ref)
    q_in = load(4, q_hbm, q_ref)

    length = len_ref[0]
    base = y * ROWS
    pick_mask = half(lax.rem(iota((ROWS, D), 0), STEP) == iota((ROWS, D), 1) // HD)
    squeeze = half(iota((PICK, ROWS), 1) // STEP == iota((PICK, ROWS), 0))

    def compact(rows):
        return nn(squeeze, rows * pick_mask).astype(bf16)

    k_in.wait()
    k_sel = compact(k_ref[...])
    v_in.wait()
    v_sel = compact(v_ref[...])
    for l in ORDER:
        kv_all[l, y, 0] = columns(k_sel, l)
        kv_all[l, y, 1] = columns(v_sel, l)

    pl.semaphore_wait(barrier, greeted)

    kv_copies = {}
    for l in ORDER:
        kv_copies[l] = [
            send(
                kv_all.at[l, y], kv_all.at[l, y], kv_s.at[l, d - 1], kv_r.at[l, d - 1], y_peer(d)
            )
            for d in FAR_FIRST
        ]
    gy_in.wait()
    gyt[0] = gy_ref[...].T
    gyt_copy = send(gyt.at[0], gyt.at[1], core_s.at[3], core_r.at[3], sibling)

    w_in.wait()
    grad[...] = nt(gy_ref[...], w_ref[...]).astype(bf16)
    q_in.wait()
    q_sel = compact(q_ref[...]) * SCALE
    g_sel = compact(grad[...])
    qg_all[y, 0] = q_sel
    qg_all[y, 1] = g_sel

    key_ok = base + iota((ROWS, 1), 0) < length
    query_at = iota((1, ROWS), 1)
    query_ok = base + query_at < length

    def dense(l):
        def pair(n, carry):
            p = l + 3 * n
            cols = pl.ds(pl.multiple_of(p * 128, 128), 128)
            k2, v2, q2, g2 = k_ref[:, cols], v_ref[:, cols], q_ref[:, cols] * SCALE, grad[:, cols]
            vt, kt = v2.T, (k2 * SCALE).T
            gk2 = jnp.zeros((ROWS, 128), f32)
            gv2 = jnp.zeros((ROWS, 128), f32)
            tops = []
            for e in range(2):
                lanes = half(iota((1, 128), 1) // HD == e)
                own = slice(e * HD, (e + 1) * HD)
                q_one, g_one = q2 * lanes, g2 * lanes
                score = jnp.where(key_ok, nt(k2, q_one), NEG)
                ex = jnp.exp(score - jnp.max(score, axis=0, keepdims=True))
                total = jnp.sum(ex, axis=0, keepdims=True)
                used = query_ok & (lax.rem(query_at, STEP) != 2 * p + e)
                prob = ex * jnp.where(used, 1.0 / total, 0.0)
                prob_half = prob.astype(bf16)
                term = prob * nt(v2, g_one)
                dot = jnp.sum(term, axis=0, keepdims=True)
                dscore = (term - prob * dot).astype(bf16)
                tops.append((nn(vt[own], prob_half), nn(kt[own], dscore)))
                gk2 = gk2 + nn(dscore, q_one)
                gv2 = gv2 + nn(prob_half, g_one)
            att[:, cols] = jnp.concatenate([tops[0][0], tops[1][0]], axis=0).T
            gq_ref[:, cols] = jnp.concatenate([tops[0][1], tops[1][1]], axis=0).T.astype(bf16)
            gk_acc[:, cols] = gk2
            gv_acc[:, cols] = gv2
            return carry

        lax.fori_loop(0, 2, pair, 0)

    diagonal = half(iota((COMPACT, 256), 0) // PICK == iota((COMPACT, 256), 1) // HD)
    row = iota((COMPACT, 1), 0)
    lane = iota((COMPACT, 128), 1)
    col = iota((ROWS, COMPACT), 1)

    def head_at(l, at):
        return 2 * l + lax.rem(at // PICK, 2) + 6 * (at // (2 * PICK))

    def block(rows):
        return jnp.concatenate([rows] * 4, axis=0) * diagonal

    def spread(l):
        at = iota((ROWS, COMPACT), 0)
        return half((at // STEP == lax.rem(col, PICK)) & (lax.rem(at, STEP) == head_at(l, col)))

    def place(l, rows):
        return nn(spread(l), rows.astype(bf16) * diagonal)

    def oks(l):
        sel_ok = base + lax.rem(row, PICK) * STEP + head_at(l, row) < length
        far_at = lane // PICK * ROWS + lax.rem(lane, PICK) * STEP + head_at(l, row)
        return sel_ok, far_at < length

    def forward(l):
        sel_ok, far_ok = oks(l)
        q_blk, g_blk = block(columns(q_sel, l)), block(columns(g_sel, l))
        k_near, v_near = columns(k_ref, l), columns(v_ref, l)
        near_score = jnp.where(query_ok, nt(q_blk, k_near), NEG)
        near_top = jnp.max(near_score, axis=1, keepdims=True)
        near_ex = jnp.exp(near_score - near_top)
        near_total = jnp.sum(near_ex, axis=1, keepdims=True)
        near_att = nn(near_ex.astype(bf16), v_near)
        near_dprob = nt(g_blk, v_near)
        spread_l = spread(l)
        dense_att = columns(att, l)
        for copy in kv_copies[l]:
            copy.wait_recv()
        k_far = kv_all[l, :, 0].reshape(FAR, 256)
        v_far = kv_all[l, :, 1].reshape(FAR, 256)
        far_score = jnp.where(far_ok, nt(q_blk, k_far), NEG)
        top = jnp.maximum(near_top, jnp.max(far_score, axis=1, keepdims=True))
        near_scale = jnp.exp(near_top - top)
        far_ex = jnp.exp(far_score - top)
        total = near_total * near_scale + jnp.sum(far_ex, axis=1, keepdims=True)
        inv = jnp.where(sel_ok, 1.0 / total, 0.0)
        near_inv = near_scale * inv
        sel_att = near_att * near_inv + nn(far_ex.astype(bf16), v_far) * inv
        attended = (dense_att + nn(spread_l, sel_att.astype(bf16) * diagonal)).astype(bf16)
        atth[l, 0] = attended[:, :128]
        atth[l, 1] = attended[:, 128:]
        copy = send(atth.at[l, 1 - c], att_far.at[l], core_s.at[l], core_r.at[l], sibling)
        near_prob, far_prob = near_ex * near_inv, far_ex * inv
        near_term = near_prob * near_dprob
        far_term = far_prob * nt(g_blk, v_far)
        dot = jnp.sum(near_term, axis=1, keepdims=True) + jnp.sum(far_term, axis=1, keepdims=True)
        aug = jnp.zeros((COMPACT, 128), f32)
        for at, left in ((0, jnp.where(sel_ok, top + jnp.log(total), 0.0)), (3, dot)):
            for n in range(3):
                top_bits = left.astype(bf16).astype(f32)
                aug = jnp.where(lane == (at + n) * STEP + head_at(l, row), top_bits, aug)
                left = left - top_bits
        aug = jnp.sum(aug.reshape(4, PICK, 128), axis=0)
        near_ds = (near_term - near_prob * dot).astype(bf16)
        far_ds = (far_term - far_prob * dot).astype(bf16)
        return copy, attended, aug, (q_blk, g_blk, near_prob, near_ds, far_ds)

    def weight(l, copy):
        total = nn(gyt[0], atth[l, c])
        copy.wait_recv()
        total = total + nn(gyt[1], att_far[l])
        w_full[l] = total.reshape(NZ, NX, 24, 128)
        if l == 1:
            wz[...] = total.reshape(NZ, 96, 128).astype(bf16)
            return [
                send(
                    wz.at[lax.rem(z + d, NZ)], r1z.at[d - 1], z_s.at[d - 1], z_r.at[d - 1], z_peer(d)
                )
                for d in FAR_FIRST
            ]
        n = l // 2
        copies = []
        for d in (2, 1, 3):
            to = lax.rem(x + d, NX)
            wx[n, to] = w_full[l, :, to].reshape(192, 128).astype(bf16)
            copies.append(
                send(wx.at[n, to], r1x.at[n, d - 1], x_s.at[n, d - 1], x_r.at[n, d - 1], x_peer(d))
            )
        return copies

    for l in ORDER:
        dense(l)
    core_0, att_0, aug_0, keep_0 = forward(0)
    core_1, att_1, aug_1, keep_1 = forward(1)
    gyt_copy.wait_recv()
    first_0 = weight(0, core_0)
    core_2, att_2, aug_2, keep_2 = forward(2)
    first_z = weight(1, core_1)
    aug_all[y] = (aug_0 + aug_1 + aug_2).astype(bf16)
    qg_copies = [
        send(qg_all.at[y], qg_all.at[y], qg_s.at[d - 1], qg_r.at[d - 1], y_peer(d))
        for d in FAR_FIRST
    ]
    aug_copies = [
        send(aug_all.at[y], aug_all.at[y], aug_s.at[d - 1], aug_r.at[d - 1], y_peer(d))
        for d in FAR_FIRST
    ]
    first_2 = weight(2, core_2)

    def put(ref, l, value):
        ref[:, 128 * l : 128 * l + 128] = value[:, :128]
        ref[:, 384 + 128 * l : 512 + 128 * l] = value[:, 128:]

    for l, keep in ((0, keep_0), (1, keep_1), (2, keep_2)):
        q_blk, g_blk, near_prob, near_ds, far_ds = keep
        k_far = kv_all[l, :, 0].reshape(FAR, 256)
        sel_gq = (nn(near_ds, columns(k_ref, l)) + nn(far_ds, k_far)) * SCALE
        put(gq_ref, l, columns(gq_ref, l) + place(l, sel_gq).astype(bf16))
        put(gk_acc, l, columns(gk_acc, l) + nn(near_ds.astype(f32).T.astype(bf16), q_blk))
        put(gv_acc, l, columns(gv_acc, l) + nn(near_prob.T.astype(bf16), g_blk))
    stores = [store(1, gq_ref, gq_hbm)]

    second_z = []
    for n, first in enumerate((first_0, first_2)):
        for copy in first:
            copy.wait_recv()
        block_sum = w_full[2 * n, :, x]
        for d in range(NX - 1):
            block_sum = block_sum + r1x[n, d].astype(f32).reshape(NZ, 24, 128)
        sum_x[n] = block_sum
        a2[n] = jnp.concatenate([block_sum, jnp.zeros((NZ, 8, 128), f32)], axis=1).astype(bf16)
        second_z.append([
            send(
                a2.at[n, lax.rem(z + d, NZ)], r22.at[n, d - 1],
                b2_s.at[n, d - 1], b2_r.at[n, d - 1], z_peer(d),
            )
            for d in FAR_FIRST
        ])

    for copy in first_z:
        copy.wait_recv()
    sum_z = w_full[1, z]
    for d in range(NZ - 1):
        sum_z = sum_z + r1z[d].astype(f32).reshape(NX, 24, 128)
    a1[...] = sum_z
    second_x = [
        send(a1.at[lax.rem(x + d, NX)], r21.at[d - 1], b1_s.at[d - 1], b1_r.at[d - 1], x_peer(d))
        for d in (2, 1, 3)
    ]
    def w_rows(l):
        return jnp.concatenate(
            [w_ref[128 * l : 128 * l + 128, :], w_ref[384 + 128 * l : 512 + 128 * l, :]], axis=0
        )

    out_ref[...] = (nn(att_0, w_rows(0)) + nn(att_1, w_rows(1)) + nn(att_2, w_rows(2))).astype(bf16)
    stores.append(store(0, out_ref, out_hbm))

    part = lax.rem(y, 4)
    last = []

    def finish(l, total):
        for c_to in range(2):
            s3[l, c_to] = total[8 * c_to : 8 * c_to + 16].astype(bf16)
        for role in range(2):
            for c_to in range(2):
                mine = (y == 4 * c + l + role) & (c == c_to)
                copy = pltpu.make_async_remote_copy(
                    src_ref=s3.at[l, c_to], dst_ref=r3.at[role, y],
                    send_sem=f_s.at[len(last)], recv_sem=f_r.at[role, y],
                    device_id=device(z, x, c_to, 4 * c + l + role), device_id_type=MESH,
                )
                last.append((copy, mine))

                @pl.when(jnp.logical_not(mine))
                def _(copy=copy):
                    copy.start()

                @pl.when(mine)
                def _(l=l, role=role, c_to=c_to):
                    r3[role, y] = s3[l, c_to]

    def finish_z(n):
        for copy in second_z[n]:
            copy.wait_recv()
        total = sum_x[n, z]
        for d in range(NZ - 1):
            total = total + r22[n, d].astype(f32)[0:24]
        finish(2 * n, total)

    finish_z(0)
    for copy in second_x:
        copy.wait_recv()
    total = a1[x]
    for d in range(NX - 1):
        total = total + r21[d]
    finish(1, total)
    finish_z(1)

    for copy in qg_copies:
        copy.wait_recv()
    for copy in aug_copies:
        copy.wait_recv()
    q_far = qg_all[:, 0].reshape(FAR, D)
    g_far = qg_all[:, 1].reshape(FAR, D)
    aug_far = aug_all[...].reshape(FAR, 128)
    for l in range(3):
        sel_ok, far_ok = oks(l)
        takes = lax.rem(lane, STEP) == head_at(l, row)
        minus_lse = jnp.where(takes & (lane < 3 * STEP), -1.0, 0.0).astype(bf16)
        minus_dot = jnp.where(takes & (lane >= 3 * STEP) & (lane < 6 * STEP), -1.0, 0.0).astype(bf16)
        q_l, g_l = columns(q_far, l), columns(g_far, l)
        own_score = nt(block(columns(k_sel, l)), q_l) + nt(minus_lse, aug_far)
        own_prob = jnp.exp(jnp.where(far_ok & sel_ok, own_score, NEG))
        own_ds = own_prob * (nt(block(columns(v_sel, l)), g_l) + nt(minus_dot, aug_far))
        gk_l = columns(gk_acc, l) + place(l, nn(own_ds.astype(bf16), q_l))
        gv_l = columns(gv_acc, l) + place(l, nn(own_prob.astype(bf16), g_l))
        put(gk_ref, l, gk_l.astype(bf16))
        put(gv_ref, l, gv_l.astype(bf16))
    stores.append(store(2, gk_ref, gk_hbm))
    stores.append(store(3, gv_ref, gv_hbm))

    sent = kv_copies[0] + kv_copies[1] + kv_copies[2] + qg_copies + aug_copies
    sent += [gyt_copy, core_0, core_1, core_2] + first_z + first_0 + first_2
    for copy in sent + second_x + second_z[0] + second_z[1]:
        copy.wait_send()
    for copy in stores:
        copy.wait()

    for copy, mine in last:

        @pl.when(jnp.logical_not(mine))
        def _(copy=copy):
            copy.wait_send()

    for role in range(2):

        @pl.when((part < role) | (part > role + 2))
        def _(role=role):
            r3[role] = jnp.zeros((NY, 16, 128), bf16)

        for at in range(NY):

            @pl.when((part >= role) & (part <= role + 2) & jnp.logical_not((y == at) & (c == y // 4)))
            def _(role=role, at=at):
                pltpu.make_async_remote_copy(
                    src_ref=s3.at[0, 0], dst_ref=r3.at[role, at],
                    send_sem=f_s.at[0], recv_sem=f_r.at[role, at],
                    device_id=device(z, x, y // 4, at), device_id_type=MESH,
                ).wait_recv()

    both = jnp.sum(r3[...].astype(f32), axis=1)
    lanes = jnp.concatenate([both[1], both[0]], axis=1)
    mine_lanes = lanes[:, 128:224]
    for t in range(1, 4):
        mine_lanes = jnp.where(part == t, lanes[:, 128 - 32 * t : 224 - 32 * t], mine_lanes)
    wg_ref[...] = jnp.where(c == 0, mine_lanes[0:12], mine_lanes[4:16])


def hand_over(*refs):
    copies = [
        pltpu.make_async_copy(src, dst, refs[10].at[n])
        for n, (src, dst) in enumerate(zip(refs[:5], refs[5:10]))
    ]
    for copy in copies:
        copy.start()
    for copy in copies:
        copy.wait()


def body(queries, keys, values, grad_y, lengths, w_out):
    hbm = pl.BlockSpec(memory_space=pltpu.HBM)
    anywhere = pl.BlockSpec(memory_space=pl.ANY)
    rows = jax.ShapeDtypeStruct((ROWS, D), bf16)
    dma = pltpu.SemaphoreType.DMA
    shapes = (rows, rows, rows, rows, jax.ShapeDtypeStruct((12, 96), f32))
    limit = 209 * 1024 * 1024 // 4
    results = pl.pallas_call(
        kernel,
        out_shape=shapes,
        in_specs=[pl.BlockSpec(memory_space=pltpu.SMEM)] + [hbm] * 5,
        out_specs=(anywhere,) * 4 + (pl.BlockSpec(memory_space=pltpu.VMEM),),
        scratch_shapes=[
            pltpu.VMEM((ROWS, D), bf16),
            pltpu.VMEM((ROWS, D), bf16),
            pltpu.VMEM((ROWS, D), bf16),
            pltpu.VMEM((ROWS, D), bf16),
            pltpu.VMEM((D, D), bf16),
            pltpu.VMEM((ROWS, D), bf16),
            pltpu.VMEM((ROWS, D), bf16),
            pltpu.VMEM((ROWS, D), bf16),
            pltpu.VMEM((ROWS, D), bf16),
            pltpu.VMEM((3, NY, 2, PICK, 256), bf16),
            pltpu.VMEM((NY, 2, PICK, D), bf16),
            pltpu.VMEM((NY, PICK, 128), bf16),
            pltpu.VMEM((2, D, ROWS), bf16),
            pltpu.VMEM((3, 2, ROWS, 128), bf16),
            pltpu.VMEM((3, ROWS, 128), bf16),
            pltpu.VMEM((ROWS, D), bf16),
            pltpu.VMEM((ROWS, D), f32),
            pltpu.VMEM((ROWS, D), f32),
            pltpu.VMEM((ROWS, D), f32),
            pltpu.VMEM((3, NZ, NX, 24, 128), f32),
            pltpu.VMEM((NZ, 96, 128), bf16),
            pltpu.VMEM((2, NX, 192, 128), bf16),
            pltpu.VMEM((NZ - 1, 96, 128), bf16),
            pltpu.VMEM((2, NX - 1, 192, 128), bf16),
            pltpu.VMEM((2, NZ, 24, 128), f32),
            pltpu.VMEM((NX, 24, 128), f32),
            pltpu.VMEM((2, NZ, 32, 128), bf16),
            pltpu.VMEM((NX - 1, 24, 128), f32),
            pltpu.VMEM((2, NZ - 1, 32, 128), bf16),
            pltpu.VMEM((3, 2, 16, 128), bf16),
            pltpu.VMEM((2, NY, 16, 128), bf16),
            dma((5,)),
            dma((4,)),
        ]
        + [dma((3, NY - 1))] * 2
        + [dma((NY - 1,))] * 4
        + [dma((4,))] * 2
        + [dma((NZ - 1,))] * 2
        + [dma((2, NX - 1))] * 2
        + [dma((NX - 1,))] * 2
        + [dma((2, NZ - 1))] * 2
        + [dma((12,)), dma((2, NY))],
        compiler_params=pltpu.CompilerParams(
            collective_id=0, has_side_effects=True, vmem_limit_bytes=limit
        ),
    )(lengths, queries, keys, values, grad_y, w_out)
    *grads, weight = pl.pallas_call(
        hand_over,
        out_shape=shapes,
        in_specs=[anywhere] * 5,
        out_specs=(hbm,) * 5,
        scratch_shapes=[dma((5,))],
        compiler_params=pltpu.CompilerParams(vmem_limit_bytes=limit),
    )(*results)
    return (*grads, weight.T)


def solution(mesh):
    split = P(("slide", "seq"), None)
    return jax.shard_map(
        body,
        mesh=mesh,
        in_specs=(split, split, split, split, P("slide"), P()),
        out_specs=(split, split, split, split, P("seq", "slide")),
        check_vma=False,
    )
```
